512 devices in a mesh: gx: 64 (over z, x, core), gy: 8 (over y).
Axes of the slice: x: 4, y: 8, z: 8, core: 2. Of those that a mesh axis runs over, the one named last changes fastest.
Arguments:
- velocity: float32 [3, 256, 128, 256], P(None, 'gx', 'gy'), may hold values from -6 to 6
- owner_brick: int32 [65536], P(('gx', 'gy')), may hold values from 0 to 255
- particle_flags: int32 [65536], P(('gx', 'gy')), may hold values from 0 to 2, as said below
- weights: float32 [65536, 128], P(('gx', 'gy')), may hold values from 0 to 0.03125
- target_velocity: float32 [3, 65536], P(None, ('gx', 'gy')), may hold values from -6 to 6
- contact_force: float32 [3, 65536], P(None, ('gx', 'gy')), may hold values from -60 to 60
Outputs:
- velocity_new: float32 [3, 256, 128, 256], P(None, 'gx', 'gy')
- pressure_potential: float32 [256, 128, 256], P('gx', 'gy')
- particle_impulse: float32 [3, 65536], P(None, ('gx', 'gy'))
The draws below stay inside these ranges and needn't reach their ends.
Inputs may be any that keep to these rules, and one draw needn't show every extreme that they name: `particle_flags`: 0 marks an empty slot, 1 a particle whose support is its owner brick, 2 one whose support also covers its next brick; at least 32 slots of each device are live, and on some device all 128 are.
All inputs are finite; a program needn't handle non-finite values.
Results may differ from the reference program's by a relative error of at most 0.0003.
Values sent between devices are 32-bit elements; how exact they have to be, the bound alone decides.
A program may use at most 64 MiB of HBM per device.

```python
import math
import jax
import jax.numpy as jnp

CX = 4
CY = 16
NZ = 256
P_DEV = 128
NX = 256
NY = 128
PARTICLES = 65536
N_GY = 8


def draw_particle_flags(key, part):
    devices_count = PARTICLES // P_DEV
    key_count, key_full, key_cross = jax.random.split(key, 3)
    counts = jax.random.randint(key_count, (devices_count,), P_DEV // 4, P_DEV + 1)
    fullest = jax.random.randint(key_full, (), 0, devices_count)
    counts = jnp.where(jnp.arange(devices_count) == fullest, P_DEV, counts)
    slot_index = jnp.arange(PARTICLES, dtype=jnp.int32)
    live_mask = slot_index % P_DEV < counts[slot_index // P_DEV]
    crossing = jax.random.randint(key_cross, (PARTICLES,), 0, 2)
    return jnp.where(live_mask, 1 + crossing, 0).astype(jnp.int32)


def with_ends(values, key, smallest, largest):
    spot = [jax.random.randint(jax.random.fold_in(key, axis), (), 0, length) for axis, length in enumerate(values.shape)]
    main_axis = values.shape.index(max(values.shape))
    beside = spot[:main_axis] + [(spot[main_axis] + 1) % values.shape[main_axis]] + spot[main_axis + 1:]
    return values.at[tuple(spot)].set(smallest).at[tuple(beside)].set(largest)


def steps_of(stream_key, shape, cuts, least, top_value):
    def one(dim, parts):
        draws = jax.random.uniform(jax.random.fold_in(jax.random.fold_in(stream_key, 6), dim), (parts,), jnp.float32, least / len(cuts), top_value / len(cuts))
        return jnp.repeat(jnp.exp(draws), shape[dim] // parts).reshape((-1,) + (1,) * (len(shape) - dim - 1))

    gain = one(*cuts[0])
    for cut in cuts[1:]:
        gain = gain * one(*cut)
    return gain


def normal_values(stream_key, extent, scale, limit, cuts=(), kind=jnp.bfloat16):
    array = scale * jax.random.normal(stream_key, extent, jnp.float32)
    if cuts:
        array = array * steps_of(stream_key, extent, cuts, -0.22, 0.18)
    return jnp.clip(array, -limit, limit).astype(kind)


def setup_inputs(seed: int = 0) -> dict:
    splits = jax.random.split(jax.random.key(seed), 7)
    return {
        "velocity": normal_values(splits[0], (3, NX, NY, NZ), 1.0, 6.0, ((1, 64), (2, 8)), jnp.float32),
        "owner_brick": with_ends(jax.random.randint(splits[1], (PARTICLES,), 0, (CX // 4) * (CY // 4) * (NZ // 4)), jax.random.fold_in(splits[1], 1), 0, ((CX // 4) * (CY // 4) * (NZ // 4)) - 1).astype(jnp.int32),
        "particle_flags": draw_particle_flags(jax.random.fold_in(splits[6], 71), 0),
        "weights": jnp.clip(0.03125 * jax.random.uniform(splits[3], (PARTICLES, 128), jnp.float32) ** steps_of(splits[3], (PARTICLES, 128), ((0, 512),), -0.2, 0.2), 0.0, 0.03125),
        "target_velocity": normal_values(splits[4], (3, PARTICLES), 1.0, 6.0, ((1, 512),), jnp.float32),
        "contact_force": normal_values(splits[5], (3, PARTICLES), 10.0, 60.0, ((1, 512),), jnp.float32),
    }


time_step = 0.05
viscosity = 2.0
volume_ratio = 16.0


def masked_sine(wavenumber, length):
    vanish = (wavenumber == 0) | (2 * wavenumber == length)
    return jnp.where(vanish, 0.0, jnp.sin(wavenumber.astype(jnp.float32) * (2.0 * math.pi / length)))


def to_bricks(grid_field):
    components, size_x, size_y, size_z = grid_field.shape
    blocks = grid_field.reshape(components, size_x // 4, 4, size_y // 4, 4, size_z // 4, 4)
    blocks = blocks.transpose(0, 1, 3, 5, 2, 4, 6)
    return blocks.reshape(components, (size_x // 4) * (size_y // 4) * (size_z // 4), 64)


def from_bricks(blocks, size_x, size_y, size_z):
    components = blocks.shape[0]
    grid_field = blocks.reshape(components, size_x // 4, size_y // 4, size_z // 4, 4, 4, 4)
    grid_field = grid_field.transpose(0, 1, 4, 2, 5, 3, 6)
    return grid_field.reshape(components, size_x, size_y, size_z)


def central(grid_field, axis_number):
    return (jnp.roll(grid_field, -1, axis_number) - jnp.roll(grid_field, 1, axis_number)) * 0.5


def spread_terms(impulse, weight):
    return (impulse.T[:, :, None] * weight[:, None, :]).reshape(weight.shape[0], 192)


def reference(velocity, owner_brick, particle_flags, weights, target_velocity, contact_force):
    laplace = -6.0 * velocity
    carried = jnp.zeros_like(velocity)
    for direction in range(3):
        upper_cell = jnp.roll(velocity, -1, direction + 1)
        lower_cell = jnp.roll(velocity, 1, direction + 1)
        laplace = laplace + upper_cell + lower_cell
        carried = carried + velocity[direction][None] * (upper_cell - lower_cell) * 0.5
    velocity_star = velocity + time_step * (viscosity * laplace - carried)

    bricks_x = CX // 4
    bricks_y = CY // 4
    bricks_z = NZ // 4
    global_x = NX // 4
    global_y = NY // 4
    total_bricks = global_x * global_y * bricks_z
    device = jnp.arange(PARTICLES, dtype=jnp.int32) // P_DEV
    index_x = device // N_GY
    index_y = device % N_GY
    brick_x = index_x * bricks_x + owner_brick // (bricks_y * bricks_z)
    brick_y = index_y * bricks_y + (owner_brick // bricks_z) % bricks_y
    brick_z = owner_brick % bricks_z
    own_index = ((brick_x * global_y + brick_y) * bricks_z + brick_z).astype(jnp.int32)
    next_index = ((((brick_x + 1) % global_x) * global_y + brick_y) * bricks_z + brick_z).astype(jnp.int32)

    live_mask = (particle_flags > 0).astype(jnp.float32)
    crossing = (particle_flags == 2).astype(jnp.float32)
    own_weight = weights[:, :64] * live_mask[:, None]
    next_weight = weights[:, 64:] * crossing[:, None]

    star_bricks = to_bricks(velocity_star)
    interpolated = jnp.sum(star_bricks[:, own_index] * own_weight[None], axis=2)
    interpolated = interpolated + jnp.sum(star_bricks[:, next_index] * next_weight[None], axis=2)
    particle_impulse = live_mask[None] * (target_velocity - interpolated + time_step * contact_force)

    spread = jax.ops.segment_sum(spread_terms(particle_impulse, own_weight), own_index, num_segments=total_bricks)
    spread = spread + jax.ops.segment_sum(spread_terms(particle_impulse, next_weight), next_index, num_segments=total_bricks)
    spread_field = from_bricks(spread.reshape(total_bricks, 3, 64).transpose(1, 0, 2), NX, NY, NZ)
    velocity_forced = velocity_star + volume_ratio * spread_field

    divergence = central(velocity_forced[0], 0) + central(velocity_forced[1], 1) + central(velocity_forced[2], 2)
    sine_x = masked_sine(jnp.arange(NX, dtype=jnp.int32), NX)[:, None, None]
    sine_y = masked_sine(jnp.arange(NY, dtype=jnp.int32), NY)[None, :, None]
    sine_z = masked_sine(jnp.arange(NZ, dtype=jnp.int32), NZ)[None, None, :]
    symbol_sum = sine_x * sine_x + sine_y * sine_y + sine_z * sine_z
    positive = symbol_sum > 0
    divergence_hat = jnp.fft.fftn(divergence)
    potential_hat = jnp.where(positive, -divergence_hat / jnp.where(positive, symbol_sum, 1.0), 0.0)
    pressure_potential = jnp.real(jnp.fft.ifftn(potential_hat)).astype(jnp.float32)
    gradient = jnp.stack([central(pressure_potential, 0), central(pressure_potential, 1), central(pressure_potential, 2)])
    velocity_new = velocity_forced - gradient
    return (velocity_new, pressure_potential, particle_impulse)
```

```python
import jax
import jax.numpy as jnp
import ml_dtypes
import numpy as np
from jax import lax
from jax.experimental import pallas as pl
from jax.experimental.pallas import tpu as pltpu
from jax.sharding import PartitionSpec as P

time_step = 0.05
viscosity = 2.0
volume_ratio = 16.0


def padded_2(cells, sides, width):
    for axis, dim in sides:
        count = lax.axis_size(axis)
        head = lax.slice_in_dim(cells, 0, width, axis=dim)
        tail = lax.slice_in_dim(cells, cells.shape[dim] - width, cells.shape[dim], axis=dim)
        cells = jnp.concatenate(
            [
                lax.ppermute(tail, axis, [(i, (i + 1) % count) for i in range(count)]),
                cells,
                lax.ppermute(head, axis, [((i + 1) % count, i) for i in range(count)]),
            ],
            axis=dim,
        )
    return cells


def shifted(array, axis, by):
    devices = lax.axis_size(axis)
    return lax.ppermute(array, axis, [(i, (i + by) % devices) for i in range(devices)])


def to_bricks(grid_field):
    components, size_x, size_y, size_z = grid_field.shape
    blocks = grid_field.reshape(components, size_x // 4, 4, size_y // 4, 4, size_z // 4, 4)
    blocks = blocks.transpose(0, 1, 3, 5, 2, 4, 6)
    return blocks.reshape(components, size_x // 4 * (size_y // 4) * (size_z // 4), 64)


def from_bricks(blocks, size_x, size_y, size_z):
    components = blocks.shape[0]
    grid_field = blocks.reshape(components, size_x // 4, size_y // 4, size_z // 4, 4, 4, 4)
    grid_field = grid_field.transpose(0, 1, 4, 2, 5, 3, 6)
    return grid_field.reshape(components, size_x, size_y, size_z)


def spread_terms(impulse, weight):
    return (impulse.T[:, :, None] * weight[:, None, :]).reshape(weight.shape[0], 192)


MESH = pl.DeviceIdType.MESH
GX, GY = 64, 8


def cas_table(points):
    index = np.arange(points)
    angle = 2.0 * np.pi * (np.outer(index, index) % points) / points
    return (np.cos(angle) + np.sin(angle)) / np.sqrt(points)


def in_two(table):
    top = table.astype(np.float32).astype(ml_dtypes.bfloat16)
    rest = (table - top.astype(np.float64)).astype(ml_dtypes.bfloat16)
    return np.stack([top, rest])


def build_tables():
    cas_128, cas_64 = cas_table(128), cas_table(64)
    depth = np.zeros((256, 256))
    for pz in range(2):
        depth[pz::2, pz * 128 : pz * 128 + 128] = cas_128
    rows = np.zeros((2, 64, 3, 8, 32))
    for py in range(2):
        for t in range(8):
            edge = (8 * t - 1) % 64 if py else (8 * t + 8) % 64
            for xi in range(3):
                rows[py, :, xi, t, 8 * xi : 8 * xi + 8] = cas_64[:, 8 * t : 8 * t + 8]
                rows[py, :, xi, t, 24 + xi] = cas_64[:, edge]
    rows = rows.reshape(2, 192, 256)
    columns = np.zeros((2, 128, 64, 3))
    for px in range(2):
        for xi in range(3):
            columns[px, :, :, xi] = cas_128[:, (2 * np.arange(64) + xi - px) % 128]
    columns = columns.reshape(2, 128, 192)

    def both(tables):
        return np.stack([in_two(table) for table in tables])

    square_128 = np.sin(np.pi * np.arange(128) / 128) ** 2
    square_64 = np.sin(np.pi * np.arange(64) / 64) ** 2
    symbol_xz = (square_128[:, None] + square_128[None, :]).astype(np.float32)
    symbol_y = np.broadcast_to(square_64[:, None], (64, 128)).astype(np.float32)
    return (
        in_two(depth),
        in_two(depth.T),
        both(rows),
        both(rows.transpose(0, 2, 1)),
        both(columns),
        both(columns.transpose(0, 2, 1)),
        symbol_xz,
        symbol_y,
    )


def halves(values):
    top = values.astype(jnp.bfloat16)
    rest = (values - top.astype(jnp.float32)).astype(jnp.bfloat16)
    return top, rest


def dot(left, right):
    return jnp.dot(left, right, preferred_element_type=jnp.float32)


def table_times(table, values):
    top, rest = halves(values)
    return dot(table[0], top) + (dot(table[1], top) + dot(table[0], rest))


def times_table(values, table):
    top, rest = halves(values)
    return dot(top, table[0]) + (dot(rest, table[0]) + dot(top, table[1]))


def exchange_gx(s, t, source, target, own_sem, send_sem, recv_sem):
    own = pltpu.make_async_copy(source.at[pl.ds(3 * s, 3)], target.at[pl.ds(3 * s, 3)], own_sem)
    own.start()

    def send(step, carry):
        peer = lax.rem(s + step, GX)
        pltpu.make_async_remote_copy(
            src_ref=source.at[pl.ds(3 * peer, 3)],
            dst_ref=target.at[pl.ds(3 * s, 3)],
            send_sem=send_sem,
            recv_sem=recv_sem,
            device_id=(peer, t),
            device_id_type=MESH,
        ).start()
        return carry

    lax.fori_loop(1, GX, send, 0)
    own.wait()
    moved = pl.ds(0, 3 * (GX - 1))
    pltpu.make_async_copy(source.at[moved], target.at[moved], recv_sem).wait()
    pltpu.make_async_copy(source.at[moved], target.at[moved], send_sem).wait()


def exchange_gy(s, t, source, target, own_sem, send_sem, recv_sem):
    own = pltpu.make_async_copy(source.at[pl.ds(32 * t, 32)], target.at[pl.ds(32 * t, 32)], own_sem)
    own.start()

    def send(step, carry):
        peer = lax.rem(t + step, GY)
        pltpu.make_async_remote_copy(
            src_ref=source.at[pl.ds(32 * peer, 27)],
            dst_ref=target.at[pl.ds(32 * t, 27)],
            send_sem=send_sem,
            recv_sem=recv_sem,
            device_id=(s, peer),
            device_id_type=MESH,
        ).start()
        return carry

    lax.fori_loop(1, GY, send, 0)
    own.wait()
    moved = pl.ds(0, 27 * (GY - 1))
    pltpu.make_async_copy(source.at[moved], target.at[moved], recv_sem).wait()
    pltpu.make_async_copy(source.at[moved], target.at[moved], send_sem).wait()


def place_of(px, xi):
    return 2 * xi + 1 - px


def put(padded, start, size, values, stride=None):
    padded[0, pl.ds(start, size, stride)] = values[:, :128]
    padded[1, pl.ds(start, size, stride)] = values[:, 128:]


def take(padded, start, size, stride=None):
    return jnp.concatenate(
        [padded[half, pl.ds(start, size, stride)] for half in range(2)], axis=1
    )


def project_kernel(
    forced,
    depth_hbm,
    depth_back_hbm,
    rows_hbm,
    rows_back_hbm,
    columns_hbm,
    columns_back_hbm,
    symbol_xz,
    symbol_y,
    velocity_new,
    potential,
    depth,
    depth_back,
    rows,
    rows_back,
    columns,
    columns_back,
    padded,
    classes,
    line_out,
    line_in,
    y_out,
    x_in,
    x_out,
    y_in,
    line_back,
    line_home,
    table_sem,
    own_sem,
    send_sem,
    recv_sem,
):
    s = lax.axis_index("gx")
    t = lax.axis_index("gy")
    px = t // 4
    py = lax.rem(t // 2, 2)
    loads = [
        pltpu.make_async_copy(source, target, table_sem.at[number])
        for number, (source, target) in enumerate(
            (
                (depth_hbm, depth),
                (depth_back_hbm, depth_back),
                (rows_hbm.at[py], rows),
                (rows_back_hbm.at[py], rows_back),
                (columns_hbm.at[px], columns),
                (columns_back_hbm.at[px], columns_back),
            )
        )
    ]
    for load in loads:
        load.start()
    line_in[...] = jnp.zeros_like(line_in)
    barrier = pltpu.get_barrier_semaphore()

    def greet_gx(step, carry):
        pl.semaphore_signal(
            barrier, inc=1, device_id=(lax.rem(s + step, GX), t), device_id_type=MESH
        )
        return carry

    def greet_gy(step, carry):
        pl.semaphore_signal(
            barrier, inc=1, device_id=(s, lax.rem(t + step, GY)), device_id_type=MESH
        )
        return carry

    lax.fori_loop(1, GY, greet_gy, 0)
    lax.fori_loop(1, GX, greet_gx, 0)

    classes[...] = jnp.zeros_like(classes)
    row_number = lax.broadcasted_iota(jnp.int32, (16, 256), 0)
    for place in range(6):
        x = place - 1
        total = jnp.zeros((16, 256), jnp.float32)
        if 0 <= x + 1 < 4:
            total = total + forced[0, x + 1]
        if 0 <= x - 1 < 4:
            total = total - forced[0, x - 1]
        if 0 <= x < 4:
            v = forced[1, x]
            w = forced[2, x]
            upper = jnp.where(row_number == 15, 0.0, pltpu.roll(v, 15, 0))
            lower = jnp.where(row_number == 0, 0.0, pltpu.roll(v, 1, 0))
            total = total + (upper - lower)
            total = total + (pltpu.roll(w, 255, 1) - pltpu.roll(w, 1, 1))
            put(padded, 32 * place + 7, 1, 0.5 * forced[1, x, 0:1])
            put(padded, 32 * place + 24, 1, -0.5 * forced[1, x, 15:16])
        else:
            put(padded, 32 * place + 7, 1, jnp.zeros((1, 256), jnp.float32))
            put(padded, 32 * place + 24, 1, jnp.zeros((1, 256), jnp.float32))
        put(padded, 32 * place + 8, 16, 0.5 * total)
    for a in range(2):
        for b in range(2):
            base = 32 * (2 * a + b)
            for xi in range(3):
                place = 32 * place_of(a, xi)
                classes[base + 8 * xi : base + 8 * xi + 8] = take(padded, place + 8 + b, 8, 2)
                edge = place + (7 if b else 24)
                classes[base + 24 + xi : base + 25 + xi] = take(padded, edge, 1)
    loads[0].wait()
    spectrum = times_table(classes[...], depth)
    for c in range(8):
        line_out[32 * c : 32 * c + 32] = spectrum[
            32 * (c // 2) : 32 * (c // 2) + 32, 128 * (c % 2) : 128 * (c % 2) + 128
        ]
    pl.semaphore_wait(barrier, GX - 1 + GY - 1)
    exchange_gy(s, t, line_out, line_in, own_sem.at[0], send_sem.at[0], recv_sem.at[0])

    loads[2].wait()
    y_out[...] = table_times(rows, line_in[...])
    exchange_gx(s, t, y_out, x_in, own_sem.at[1], send_sem.at[1], recv_sem.at[1])

    loads[4].wait()
    loads[5].wait()
    symbol = symbol_xz[...] + symbol_y[pl.ds(s, 1)]
    positive = symbol > 0
    factor = jnp.where(positive, -1.0 / jnp.where(positive, symbol, 1.0), 0.0)
    x_out[...] = table_times(columns_back, table_times(columns, x_in[...]) * factor)
    exchange_gx(s, t, x_out, y_in, own_sem.at[2], send_sem.at[2], recv_sem.at[2])

    loads[3].wait()
    line_back[...] = table_times(rows_back, y_in[...])
    exchange_gy(s, t, line_back, line_home, own_sem.at[3], send_sem.at[3], recv_sem.at[3])

    loads[1].wait()
    home = jnp.concatenate(
        [
            jnp.concatenate(
                [line_home[64 * c : 64 * c + 32], line_home[64 * c + 32 : 64 * c + 64]], axis=1
            )
            for c in range(4)
        ],
        axis=0,
    )
    classes[...] = times_table(home, depth_back)
    for a in range(2):
        for b in range(2):
            base = 32 * (2 * a + b)
            for xi in range(3):
                place = 32 * place_of(a, xi)
                put(padded, place + 8 + b, 8, classes[base + 8 * xi : base + 8 * xi + 8], 2)
                edge = place + (7 if b else 24)
                put(padded, edge, 1, classes[base + 24 + xi : base + 25 + xi])
    for x in range(4):
        base = 32 * (x + 1)
        p = take(padded, base + 8, 16)
        potential[x] = p
        velocity_new[0, x] = forced[0, x] - 0.5 * (
            take(padded, base + 40, 16) - take(padded, base - 24, 16)
        )
        velocity_new[1, x] = forced[1, x] - 0.5 * (
            take(padded, base + 9, 16) - take(padded, base + 7, 16)
        )
        velocity_new[2, x] = forced[2, x] - 0.5 * (pltpu.roll(p, 255, 1) - pltpu.roll(p, 1, 1))


def project(forced):
    tables = build_tables()
    inside = pl.BlockSpec(memory_space=pltpu.VMEM)
    anywhere = pl.BlockSpec(memory_space=pl.ANY)
    f32, bf16 = jnp.float32, jnp.bfloat16
    return pl.pallas_call(
        project_kernel,
        out_shape=(
            jax.ShapeDtypeStruct((3, 4, 16, 256), f32),
            jax.ShapeDtypeStruct((4, 16, 256), f32),
        ),
        in_specs=[inside] + [anywhere] * 6 + [inside] * 2,
        out_specs=(inside, inside),
        scratch_shapes=[
            pltpu.VMEM((2, 256, 256), bf16),
            pltpu.VMEM((2, 256, 256), bf16),
            pltpu.VMEM((2, 192, 256), bf16),
            pltpu.VMEM((2, 256, 192), bf16),
            pltpu.VMEM((2, 128, 192), bf16),
            pltpu.VMEM((2, 192, 128), bf16),
            pltpu.VMEM((2, 192, 128), f32),
            pltpu.VMEM((128, 256), f32),
            pltpu.VMEM((256, 128), f32),
            pltpu.VMEM((256, 128), f32),
            pltpu.VMEM((192, 128), f32),
            pltpu.VMEM((192, 128), f32),
            pltpu.VMEM((192, 128), f32),
            pltpu.VMEM((192, 128), f32),
            pltpu.VMEM((256, 128), f32),
            pltpu.VMEM((256, 128), f32),
            pltpu.SemaphoreType.DMA((6,)),
            pltpu.SemaphoreType.DMA((4,)),
            pltpu.SemaphoreType.DMA((4,)),
            pltpu.SemaphoreType.DMA((4,)),
        ],
        compiler_params=pltpu.CompilerParams(collective_id=0, has_side_effects=True),
    )(forced, *[jnp.asarray(table) for table in tables])


def advance(velocity):
    padded = padded_2(velocity, (("gx", 1), ("gy", 2)), 1)
    uppers = (padded[:, 2:, 1:-1], padded[:, 1:-1, 2:], jnp.roll(velocity, -1, 3))
    lowers = (padded[:, :-2, 1:-1], padded[:, 1:-1, :-2], jnp.roll(velocity, 1, 3))
    laplace = -6.0 * velocity
    carried = jnp.zeros_like(velocity)
    for direction in range(3):
        laplace = laplace + uppers[direction] + lowers[direction]
        carried = (
            carried + velocity[direction][None] * (uppers[direction] - lowers[direction]) * 0.5
        )
    return velocity + time_step * (viscosity * laplace - carried)


def body(velocity, owner_brick, particle_flags, weights, target_velocity, contact_force):
    size_x = velocity.shape[1]
    size_y = velocity.shape[2]
    size_z = velocity.shape[3]
    velocity_star = advance(velocity)
    bricks_x = size_x // 4
    layer_size = size_y // 4 * (size_z // 4)
    total_bricks = bricks_x * layer_size
    star_bricks = to_bricks(velocity_star)
    block_x = owner_brick // layer_size
    in_layer = owner_brick % layer_size
    inside = block_x < bricks_x - 1
    live_mask = (particle_flags > 0).astype(jnp.float32)
    crossing = (particle_flags == 2).astype(jnp.float32)
    own_weight = weights[:, :64] * live_mask[:, None]
    next_weight = weights[:, 64:] * crossing[:, None]
    inner_weight = next_weight * inside.astype(jnp.float32)[:, None]
    outer_weight = next_weight - inner_weight
    inner_index = jnp.where(inside, owner_brick + layer_size, owner_brick)
    interpolated = jnp.sum(star_bricks[:, owner_brick] * own_weight[None], axis=2)
    interpolated = interpolated + jnp.sum(star_bricks[:, inner_index] * inner_weight[None], axis=2)
    from_next = shifted(star_bricks, "gx", -1)
    interpolated = interpolated + jnp.sum(from_next[:, in_layer] * outer_weight[None], axis=2)
    particle_impulse = live_mask[None] * (
        target_velocity - interpolated + time_step * contact_force
    )
    outgoing = jax.ops.segment_sum(
        spread_terms(particle_impulse, outer_weight), in_layer, num_segments=layer_size
    )
    received = shifted(outgoing, "gx", 1)
    spread = jax.ops.segment_sum(
        spread_terms(particle_impulse, own_weight), owner_brick, num_segments=total_bricks
    )
    spread = spread + jax.ops.segment_sum(
        spread_terms(particle_impulse, inner_weight), inner_index, num_segments=total_bricks
    )
    spread = spread + received
    spread_field = from_bricks(
        spread.reshape(total_bricks, 3, 64).transpose(1, 0, 2), size_x, size_y, size_z
    )
    velocity_forced = velocity_star + volume_ratio * spread_field
    velocity_new, pressure_potential = project(velocity_forced)
    return (velocity_new, pressure_potential, particle_impulse)


def solution(mesh):
    placed = (
        P(None, "gx", "gy", None),
        P(("gx", "gy")),
        P(("gx", "gy")),
        P(("gx", "gy"), None),
        P(None, ("gx", "gy")),
        P(None, ("gx", "gy")),
    )
    return jax.shard_map(
        body,
        mesh=mesh,
        in_specs=placed,
        out_specs=(P(None, "gx", "gy", None), P("gx", "gy", None), P(None, ("gx", "gy"))),
        check_vma=False,
    )
```

```python
import jax
import jax.numpy as jnp
import ml_dtypes
import numpy as np
from jax import lax
from jax.experimental import pallas as pl
from jax.experimental.pallas import tpu as pltpu
from jax.sharding import PartitionSpec as P

time_step = 0.05
viscosity = 2.0
volume_ratio = 16.0

MESH = pl.DeviceIdType.MESH
GX, GY = 64, 8


def cas_table(points):
    index = np.arange(points)
    angle = 2.0 * np.pi * (np.outer(index, index) % points) / points
    return (np.cos(angle) + np.sin(angle)) / np.sqrt(points)


def in_two(table):
    top = table.astype(np.float32).astype(ml_dtypes.bfloat16)
    rest = (table - top.astype(np.float64)).astype(ml_dtypes.bfloat16)
    return np.stack([top, rest])


def build_tables():
    cas_128, cas_64 = cas_table(128), cas_table(64)
    depth = np.zeros((256, 256))
    for pz in range(2):
        depth[pz::2, pz * 128 : pz * 128 + 128] = cas_128
    rows = np.zeros((2, 64, 3, 8, 32))
    for py in range(2):
        for t in range(8):
            edge = (8 * t - 1) % 64 if py else (8 * t + 8) % 64
            for xi in range(3):
                rows[py, :, xi, t, 8 * xi : 8 * xi + 8] = cas_64[:, 8 * t : 8 * t + 8]
                rows[py, :, xi, t, 24 + xi] = cas_64[:, edge]
    rows = rows.reshape(2, 192, 256)
    columns = np.zeros((2, 128, 64, 3))
    for px in range(2):
        for xi in range(3):
            columns[px, :, :, xi] = cas_128[:, (2 * np.arange(64) + xi - px) % 128]
    columns = columns.reshape(2, 128, 192)

    n, kk, i, y = np.indices((2, 4, 4, 16)).reshape(4, 512)
    cells = np.arange(128) == (64 * n + 16 * i + 4 * (y % 4) + kk)[:, None]

    def both(tables):
        return np.stack([in_two(table) for table in tables])

    square_128 = np.sin(np.pi * np.arange(128) / 128) ** 2
    square_64 = np.sin(np.pi * np.arange(64) / 64) ** 2
    symbol_xz = (square_128[:, None] + square_128[None, :]).astype(np.float32)
    symbol_y = np.broadcast_to(square_64[:, None], (64, 128)).astype(np.float32)
    return (
        cells.astype(ml_dtypes.bfloat16),
        in_two(depth),
        in_two(depth.T),
        both(rows),
        both(rows.transpose(0, 2, 1)),
        both(columns),
        both(columns.transpose(0, 2, 1)),
        symbol_xz,
        symbol_y,
    )


def halves(values):
    top = values.astype(jnp.bfloat16)
    rest = (values - top.astype(jnp.float32)).astype(jnp.bfloat16)
    return top, rest


def dot(left, right):
    return jnp.dot(left, right, preferred_element_type=jnp.float32)


def table_times(table, values):
    top, rest = halves(values)
    return dot(table[0], top) + (dot(table[1], top) + dot(table[0], rest))


def times_table(values, table):
    top, rest = halves(values)
    return dot(top, table[0]) + (dot(rest, table[0]) + dot(top, table[1]))


def exchange_gx(s, t, source, target, own_sem, send_sem, recv_sem):
    own = pltpu.make_async_copy(source.at[pl.ds(3 * s, 3)], target.at[pl.ds(3 * s, 3)], own_sem)
    own.start()

    def send(step, carry):
        peer = lax.rem(s + step, GX)
        pltpu.make_async_remote_copy(
            src_ref=source.at[pl.ds(3 * peer, 3)],
            dst_ref=target.at[pl.ds(3 * s, 3)],
            send_sem=send_sem,
            recv_sem=recv_sem,
            device_id=(peer, t),
            device_id_type=MESH,
        ).start()
        return carry

    lax.fori_loop(1, GX, send, 0)
    own.wait()
    moved = pl.ds(0, 3 * (GX - 1))
    pltpu.make_async_copy(source.at[moved], target.at[moved], recv_sem).wait()
    pltpu.make_async_copy(source.at[moved], target.at[moved], send_sem).wait()


def exchange_gy(s, t, source, target, own_sem, send_sem, recv_sem):
    own = pltpu.make_async_copy(source.at[pl.ds(32 * t, 32)], target.at[pl.ds(32 * t, 32)], own_sem)
    own.start()

    def send(step, carry):
        peer = lax.rem(t + step, GY)
        pltpu.make_async_remote_copy(
            src_ref=source.at[pl.ds(32 * peer, 27)],
            dst_ref=target.at[pl.ds(32 * t, 27)],
            send_sem=send_sem,
            recv_sem=recv_sem,
            device_id=(s, peer),
            device_id_type=MESH,
        ).start()
        return carry

    lax.fori_loop(1, GY, send, 0)
    own.wait()
    moved = pl.ds(0, 27 * (GY - 1))
    pltpu.make_async_copy(source.at[moved], target.at[moved], recv_sem).wait()
    pltpu.make_async_copy(source.at[moved], target.at[moved], send_sem).wait()


def dot_across(left, right):
    return lax.dot_general(
        left, right, (((1,), (1,)), ((), ())), preferred_element_type=jnp.float32
    )


def spread_weights(cells, weights, bricks, shown):
    top, rest = halves(weights)
    found = dot_across(cells, top) + dot_across(cells, rest)
    row = lax.broadcasted_iota(jnp.int32, (64, 128), 0)
    mask = (lax.rem(row, 16) // 4 == bricks // 64) & shown
    return [jnp.where(mask, found[64 * k : 64 * k + 64], 0.0) for k in range(4)]


def depth_cells(bricks):
    first = 4 * lax.rem(bricks, 64)
    wanted = jnp.concatenate([first + k for k in range(4)], axis=1)
    z = lax.broadcasted_iota(jnp.int32, (256, 512), 0)
    return jnp.where(z == wanted, 1.0, 0.0).astype(jnp.bfloat16)


def spread(impulse, weights, selector):
    terms = jnp.concatenate(
        [
            jnp.concatenate([weights[k] * impulse[c : c + 1] for k in range(4)], axis=1)
            for c in range(3)
        ],
        axis=0,
    )
    top, rest = halves(terms)
    return dot_across(top, selector) + dot_across(rest, selector)


def place_of(px, xi):
    return 2 * xi + 1 - px


def put(padded, start, size, values, stride=None):
    padded[0, pl.ds(start, size, stride)] = values[:, :128]
    padded[1, pl.ds(start, size, stride)] = values[:, 128:]


def take(padded, start, size, stride=None):
    return jnp.concatenate(
        [padded[half, pl.ds(start, size, stride)] for half in range(2)], axis=1
    )


def step_kernel(
    velocity,
    bricks,
    flags,
    weights_hbm,
    target_velocity,
    contact_force,
    cells,
    depth_hbm,
    depth_back_hbm,
    rows_hbm,
    rows_back_hbm,
    columns_hbm,
    columns_back_hbm,
    symbol_xz,
    symbol_y,
    velocity_new,
    potential,
    impulse_out,
    depth,
    depth_back,
    rows,
    rows_back,
    columns,
    columns_back,
    region,
    weights,
    weights_below,
    bricks_below,
    flags_below,
    star,
    impulse,
    impulse_below,
    forced,
    padded,
    classes,
    line_out,
    line_in,
    y_out,
    x_in,
    x_out,
    y_in,
    line_back,
    line_home,
    table_sem,
    near_send,
    near_recv,
    own_sem,
    send_sem,
    recv_sem,
):
    s = lax.axis_index("gx")
    t = lax.axis_index("gy")
    px = t // 4
    py = lax.rem(t // 2, 2)
    loads = [
        pltpu.make_async_copy(source, target, table_sem.at[number])
        for number, (source, target) in enumerate(
            (
                (depth_hbm, depth),
                (depth_back_hbm, depth_back),
                (rows_hbm.at[py], rows),
                (rows_back_hbm.at[py], rows_back),
                (columns_hbm.at[px], columns),
                (columns_back_hbm.at[px], columns_back),
                (velocity, region.at[:, pl.ds(1, 4), pl.ds(8, 16)]),
                (weights_hbm, weights),
            )
        )
    ]
    for number in (6, 7, 0, 2, 4, 5, 3, 1):
        loads[number].start()
    line_in[...] = jnp.zeros_like(line_in)
    barrier = pltpu.get_barrier_semaphore()

    def away(dx, dy):
        return (lax.rem(s + GX + dx, GX), lax.rem(t + GY + dy, GY))

    def greet_gx(step, carry):
        pl.semaphore_signal(
            barrier, inc=1, device_id=(lax.rem(s + step, GX), t), device_id_type=MESH
        )
        return carry

    def greet_gy(step, carry):
        pl.semaphore_signal(
            barrier, inc=1, device_id=(s, lax.rem(t + step, GY)), device_id_type=MESH
        )
        return carry

    for dy in (-1, 1):
        pl.semaphore_signal(barrier, inc=1, device_id=away(1, dy), device_id_type=MESH)
    lax.fori_loop(1, GY, greet_gy, 0)
    lax.fori_loop(1, GX, greet_gx, 0)
    pl.semaphore_wait(barrier, GX - 1 + GY - 1 + 2)

    near = [
        pltpu.make_async_remote_copy(
            src_ref=source,
            dst_ref=target,
            send_sem=near_send.at[number],
            recv_sem=near_recv.at[number],
            device_id=away(*where),
            device_id_type=MESH,
        )
        for number, (source, target, where) in enumerate(
            (
                (velocity, region.at[:, pl.ds(5, 4), pl.ds(8, 16)], (-1, 0)),
                (velocity.at[:, pl.ds(3, 1)], region.at[:, pl.ds(0, 1), pl.ds(8, 16)], (1, 0)),
                (velocity.at[:, pl.ds(0, 1)], region.at[:, pl.ds(9, 1), pl.ds(8, 16)], (-2, 0)),
                (velocity.at[:, :, pl.ds(0, 1)], region.at[:, pl.ds(1, 4), pl.ds(24, 1)], (0, -1)),
                (velocity.at[:, :, pl.ds(0, 1)], region.at[:, pl.ds(5, 4), pl.ds(24, 1)], (-1, -1)),
                (velocity.at[:, :, pl.ds(15, 1)], region.at[:, pl.ds(1, 4), pl.ds(7, 1)], (0, 1)),
                (velocity.at[:, :, pl.ds(15, 1)], region.at[:, pl.ds(5, 4), pl.ds(7, 1)], (-1, 1)),
                (weights_hbm, weights_below, (1, 0)),
                (bricks, bricks_below, (1, 0)),
                (flags, flags_below, (1, 0)),
                (impulse, impulse_below, (1, 0)),
            )
        )
    ]
    for number in range(10):
        near[number].start()

    loads[7].wait()
    own_bricks = bricks[...]
    live = flags[...] > 0
    own_weights = spread_weights(cells[0:256], weights[...], own_bricks, live)
    next_weights = spread_weights(cells[256:512], weights[...], own_bricks, flags[...] == 2)
    selector = depth_cells(own_bricks)
    for number in (6,):
        loads[number].wait()
    for number in range(7):
        near[number].wait_recv()
    for x in range(1, 9):
        block, inner = (x - 1) // 4, (x - 1) % 4
        centers = [region[c, x, 8:24] for c in range(3)]
        for c in range(3):
            v = centers[c]
            uppers = (region[c, x + 1, 8:24], region[c, x, 9:25], pltpu.roll(v, 255, 1))
            lowers = (region[c, x - 1, 8:24], region[c, x, 7:23], pltpu.roll(v, 1, 1))
            laplace = -6.0 * v
            carried = jnp.zeros_like(v)
            for d in range(3):
                laplace = laplace + (uppers[d] + lowers[d])
                carried = carried + centers[d] * (uppers[d] - lowers[d])
            base = 192 * block + 64 * c + 16 * inner
            star[base : base + 16] = v + time_step * (viscosity * laplace - 0.5 * carried)

    top, rest = halves(star[...])
    found = dot(top, selector) + dot(rest, selector)
    for c in range(3):
        total = jnp.zeros((64, 128), jnp.float32)
        for block, part in enumerate((own_weights, next_weights)):
            base = 192 * block + 64 * c
            for k in range(4):
                total = total + found[base : base + 64, 128 * k : 128 * k + 128] * part[k]
        interpolated = jnp.sum(total, axis=0, keepdims=True)
        wanted = target_velocity[c : c + 1] + time_step * contact_force[c : c + 1]
        impulse[c : c + 1] = jnp.where(live, wanted - interpolated, 0.0)
    near[10].start()
    impulse_out[...] = impulse[...]
    at_home = spread(impulse[...], own_weights, selector)
    for number in (7, 8, 9):
        near[number].wait_recv()
    weights_from = spread_weights(
        cells[256:512], weights_below[...], bricks_below[...], flags_below[...] == 2
    )
    selector_from = depth_cells(bricks_below[...])
    near[10].wait_recv()
    from_below = spread(impulse_below[...], weights_from, selector_from)
    for c in range(3):
        for x in range(4):
            base = 64 * c + 16 * x
            forced[c, x] = star[base : base + 16] + volume_ratio * (
                at_home[base : base + 16] + from_below[base : base + 16]
            )

    classes[...] = jnp.zeros_like(classes)
    row_number = lax.broadcasted_iota(jnp.int32, (16, 256), 0)
    for place in range(6):
        x = place - 1
        total = jnp.zeros((16, 256), jnp.float32)
        if 0 <= x + 1 < 4:
            total = total + forced[0, x + 1]
        if 0 <= x - 1 < 4:
            total = total - forced[0, x - 1]
        if 0 <= x < 4:
            v = forced[1, x]
            w = forced[2, x]
            upper = jnp.where(row_number == 15, 0.0, pltpu.roll(v, 15, 0))
            lower = jnp.where(row_number == 0, 0.0, pltpu.roll(v, 1, 0))
            total = total + (upper - lower)
            total = total + (pltpu.roll(w, 255, 1) - pltpu.roll(w, 1, 1))
            put(padded, 32 * place + 7, 1, 0.5 * forced[1, x, 0:1])
            put(padded, 32 * place + 24, 1, -0.5 * forced[1, x, 15:16])
        else:
            put(padded, 32 * place + 7, 1, jnp.zeros((1, 256), jnp.float32))
            put(padded, 32 * place + 24, 1, jnp.zeros((1, 256), jnp.float32))
        put(padded, 32 * place + 8, 16, 0.5 * total)
    for a in range(2):
        for b in range(2):
            base = 32 * (2 * a + b)
            for xi in range(3):
                place = 32 * place_of(a, xi)
                classes[base + 8 * xi : base + 8 * xi + 8] = take(padded, place + 8 + b, 8, 2)
                edge = place + (7 if b else 24)
                classes[base + 24 + xi : base + 25 + xi] = take(padded, edge, 1)
    loads[0].wait()
    spectrum = times_table(classes[...], depth)
    for c in range(8):
        line_out[32 * c : 32 * c + 32] = spectrum[
            32 * (c // 2) : 32 * (c // 2) + 32, 128 * (c % 2) : 128 * (c % 2) + 128
        ]
    exchange_gy(s, t, line_out, line_in, own_sem.at[0], send_sem.at[0], recv_sem.at[0])

    loads[2].wait()
    y_out[...] = table_times(rows, line_in[...])
    exchange_gx(s, t, y_out, x_in, own_sem.at[1], send_sem.at[1], recv_sem.at[1])

    loads[4].wait()
    loads[5].wait()
    symbol = symbol_xz[...] + symbol_y[pl.ds(s, 1)]
    positive = symbol > 0
    factor = jnp.where(positive, -1.0 / jnp.where(positive, symbol, 1.0), 0.0)
    x_out[...] = table_times(columns_back, table_times(columns, x_in[...]) * factor)
    exchange_gx(s, t, x_out, y_in, own_sem.at[2], send_sem.at[2], recv_sem.at[2])

    loads[3].wait()
    line_back[...] = table_times(rows_back, y_in[...])
    exchange_gy(s, t, line_back, line_home, own_sem.at[3], send_sem.at[3], recv_sem.at[3])

    loads[1].wait()
    home = jnp.concatenate(
        [
            jnp.concatenate(
                [line_home[64 * c : 64 * c + 32], line_home[64 * c + 32 : 64 * c + 64]], axis=1
            )
            for c in range(4)
        ],
        axis=0,
    )
    classes[...] = times_table(home, depth_back)
    for a in range(2):
        for b in range(2):
            base = 32 * (2 * a + b)
            for xi in range(3):
                place = 32 * place_of(a, xi)
                put(padded, place + 8 + b, 8, classes[base + 8 * xi : base + 8 * xi + 8], 2)
                edge = place + (7 if b else 24)
                put(padded, edge, 1, classes[base + 24 + xi : base + 25 + xi])
    for x in range(4):
        base = 32 * (x + 1)
        p = take(padded, base + 8, 16)
        potential[x] = p
        velocity_new[0, x] = forced[0, x] - 0.5 * (
            take(padded, base + 40, 16) - take(padded, base - 24, 16)
        )
        velocity_new[1, x] = forced[1, x] - 0.5 * (
            take(padded, base + 9, 16) - take(padded, base + 7, 16)
        )
        velocity_new[2, x] = forced[2, x] - 0.5 * (pltpu.roll(p, 255, 1) - pltpu.roll(p, 1, 1))
    for copy in near:
        copy.wait_send()


def step(velocity, owner_brick, particle_flags, weights, target_velocity, contact_force):
    tables = build_tables()
    inside = pl.BlockSpec(memory_space=pltpu.VMEM)
    anywhere = pl.BlockSpec(memory_space=pl.ANY)
    f32, bf16 = jnp.float32, jnp.bfloat16
    return pl.pallas_call(
        step_kernel,
        out_shape=(
            jax.ShapeDtypeStruct((3, 4, 16, 256), f32),
            jax.ShapeDtypeStruct((4, 16, 256), f32),
            jax.ShapeDtypeStruct((3, 128), f32),
        ),
        in_specs=[anywhere, inside, inside, anywhere, inside, inside, inside]
        + [anywhere] * 6
        + [inside] * 2,
        out_specs=(inside, inside, inside),
        scratch_shapes=[
            pltpu.VMEM((2, 256, 256), bf16),
            pltpu.VMEM((2, 256, 256), bf16),
            pltpu.VMEM((2, 192, 256), bf16),
            pltpu.VMEM((2, 256, 192), bf16),
            pltpu.VMEM((2, 128, 192), bf16),
            pltpu.VMEM((2, 192, 128), bf16),
            pltpu.VMEM((3, 10, 32, 256), f32),
            pltpu.VMEM((128, 128), f32),
            pltpu.VMEM((128, 128), f32),
            pltpu.VMEM((1, 128), jnp.int32),
            pltpu.VMEM((1, 128), jnp.int32),
            pltpu.VMEM((384, 256), f32),
            pltpu.VMEM((3, 128), f32),
            pltpu.VMEM((3, 128), f32),
            pltpu.VMEM((3, 4, 16, 256), f32),
            pltpu.VMEM((2, 192, 128), f32),
            pltpu.VMEM((128, 256), f32),
            pltpu.VMEM((256, 128), f32),
            pltpu.VMEM((256, 128), f32),
            pltpu.VMEM((192, 128), f32),
            pltpu.VMEM((192, 128), f32),
            pltpu.VMEM((192, 128), f32),
            pltpu.VMEM((192, 128), f32),
            pltpu.VMEM((256, 128), f32),
            pltpu.VMEM((256, 128), f32),
            pltpu.SemaphoreType.DMA((8,)),
            pltpu.SemaphoreType.DMA((11,)),
            pltpu.SemaphoreType.DMA((11,)),
            pltpu.SemaphoreType.DMA((4,)),
            pltpu.SemaphoreType.DMA((4,)),
            pltpu.SemaphoreType.DMA((4,)),
        ],
        compiler_params=pltpu.CompilerParams(
            collective_id=0, has_side_effects=True, vmem_limit_bytes=32 * 1024 * 1024
        ),
    )(
        velocity,
        owner_brick.reshape(1, 128),
        particle_flags.reshape(1, 128),
        weights,
        target_velocity,
        contact_force,
        *[jnp.asarray(table) for table in tables],
    )


def solution(mesh):
    placed = (
        P(None, "gx", "gy", None),
        P(("gx", "gy")),
        P(("gx", "gy")),
        P(("gx", "gy"), None),
        P(None, ("gx", "gy")),
        P(None, ("gx", "gy")),
    )
    return jax.shard_map(
        step,
        mesh=mesh,
        in_specs=placed,
        out_specs=(P(None, "gx", "gy", None), P("gx", "gy", None), P(None, ("gx", "gy"))),
        check_vma=False,
    )
```

```python
import jax
import jax.numpy as jnp
import ml_dtypes
import numpy as np
from jax import lax
from jax.experimental import pallas as pl
from jax.experimental.pallas import tpu as pltpu
from jax.sharding import PartitionSpec as P

time_step = 0.05
viscosity = 2.0
volume_ratio = 16.0

MESH = pl.DeviceIdType.MESH
GX, GY = 64, 8


def cas_table(points):
    index = np.arange(points)
    angle = 2.0 * np.pi * (np.outer(index, index) % points) / points
    return (np.cos(angle) + np.sin(angle)) / np.sqrt(points)


def in_two(table):
    top = table.astype(np.float32).astype(ml_dtypes.bfloat16)
    rest = (table - top.astype(np.float64)).astype(ml_dtypes.bfloat16)
    return np.stack([top, rest])


def build_tables():
    cas_128, cas_64 = cas_table(128), cas_table(64)
    depth = np.zeros((256, 256))
    for pz in range(2):
        depth[pz::2, pz * 128 : pz * 128 + 128] = cas_128
    rows = np.zeros((2, 64, 3, 8, 32))
    for py in range(2):
        for t in range(8):
            edge = (8 * t - 1) % 64 if py else (8 * t + 8) % 64
            for xi in range(3):
                rows[py, :, xi, t, 8 * xi : 8 * xi + 8] = cas_64[:, 8 * t : 8 * t + 8]
                rows[py, :, xi, t, 24 + xi] = cas_64[:, edge]
    rows = rows.reshape(2, 192, 256)
    columns = np.zeros((2, 128, 64, 3))
    for px in range(2):
        for xi in range(3):
            columns[px, :, :, xi] = cas_128[:, (2 * np.arange(64) + xi - px) % 128]
    columns = columns.reshape(2, 128, 192)

    n, kk, i, y = np.indices((2, 4, 4, 16)).reshape(4, 512)
    cells = np.arange(128) == (64 * n + 16 * i + 4 * (y % 4) + kk)[:, None]

    def both(tables):
        return np.stack([in_two(table) for table in tables])

    square_128 = np.sin(np.pi * np.arange(128) / 128) ** 2
    square_64 = np.sin(np.pi * np.arange(64) / 64) ** 2
    symbol_xz = (square_128[:, None] + square_128[None, :]).astype(np.float32)
    symbol_y = np.broadcast_to(square_64[:, None], (64, 128)).astype(np.float32)
    return (
        cells.astype(ml_dtypes.bfloat16),
        in_two(depth),
        in_two(depth.T),
        both(rows),
        both(rows.transpose(0, 2, 1)),
        both(columns),
        both(columns.transpose(0, 2, 1)),
        symbol_xz,
        symbol_y,
    )


def halves(values):
    top = values.astype(jnp.bfloat16)
    rest = (values - top.astype(jnp.float32)).astype(jnp.bfloat16)
    return top, rest


def dot(left, right):
    return jnp.dot(left, right, preferred_element_type=jnp.float32)


def table_times(table, values):
    top, rest = halves(values)
    return dot(table[0], top) + (dot(table[1], top) + dot(table[0], rest))


def times_table(values, table):
    top, rest = halves(values)
    return dot(top, table[0]) + (dot(rest, table[0]) + dot(top, table[1]))


def outward(step, size):
    odd = lax.rem(step, 2)
    return size // 2 + (1 - odd) * (step // 2) - odd * ((step + 1) // 2)


def exchange_gx(s, t, source, target, own_sem, send_sem, recv_sem):
    own = pltpu.make_async_copy(source.at[pl.ds(3 * s, 3)], target.at[pl.ds(3 * s, 3)], own_sem)
    own.start()

    def send(step, carry):
        z = lax.rem(s // 8 + outward(step // 8, 8), 8)
        x = lax.rem(lax.rem(s // 2, 4) + outward(lax.rem(step // 2, 4), 4), 4)
        peer = 8 * z + 2 * x + lax.rem(s + 1 + step, 2)
        pltpu.make_async_remote_copy(
            src_ref=source.at[pl.ds(3 * peer, 3)],
            dst_ref=target.at[pl.ds(3 * s, 3)],
            send_sem=send_sem,
            recv_sem=recv_sem,
            device_id=(peer, t),
            device_id_type=MESH,
        ).start()
        return carry

    lax.fori_loop(0, GX - 1, send, 0)
    own.wait()
    moved = pl.ds(0, 3 * (GX - 1))
    pltpu.make_async_copy(source.at[moved], target.at[moved], recv_sem).wait()
    pltpu.make_async_copy(source.at[moved], target.at[moved], send_sem).wait()


def exchange_gy(s, t, source, target, own_sem, send_sem, recv_sem):
    own = pltpu.make_async_copy(source.at[pl.ds(32 * t, 32)], target.at[pl.ds(32 * t, 32)], own_sem)
    own.start()

    def send(step, carry):
        peer = lax.rem(t + outward(step, GY), GY)
        pltpu.make_async_remote_copy(
            src_ref=source.at[pl.ds(32 * peer, 27)],
            dst_ref=target.at[pl.ds(32 * t, 27)],
            send_sem=send_sem,
            recv_sem=recv_sem,
            device_id=(s, peer),
            device_id_type=MESH,
        ).start()
        return carry

    lax.fori_loop(0, GY - 1, send, 0)
    own.wait()
    moved = pl.ds(0, 27 * (GY - 1))
    pltpu.make_async_copy(source.at[moved], target.at[moved], recv_sem).wait()
    pltpu.make_async_copy(source.at[moved], target.at[moved], send_sem).wait()


def dot_across(left, right):
    return lax.dot_general(
        left, right, (((1,), (1,)), ((), ())), preferred_element_type=jnp.float32
    )


def spread_weights(cells, weights, bricks, shown):
    top, rest = halves(weights)
    found = dot_across(cells, top) + dot_across(cells, rest)
    row = lax.broadcasted_iota(jnp.int32, (64, 128), 0)
    mask = (lax.rem(row, 16) // 4 == bricks // 64) & shown
    return [jnp.where(mask, found[64 * k : 64 * k + 64], 0.0) for k in range(4)]


def both_weights(cells, weights, bricks, flags):
    parts = ((cells[0:256], flags[...] > 0), (cells[256:512], flags[...] == 2))
    return [spread_weights(part, weights[...], bricks[...], shown) for part, shown in parts]


def impulse_of(star, selector, weights, wanted, flags):
    top, rest = halves(star)
    found = dot(top, selector) + dot(rest, selector)
    interpolated = []
    for c in range(3):
        total = jnp.zeros((64, 128), jnp.float32)
        for block in range(2):
            base = 192 * block + 64 * c
            for k in range(4):
                cell = found[base : base + 64, 128 * k : 128 * k + 128]
                total = total + cell * weights[block][k]
        interpolated.append(jnp.sum(total, axis=0, keepdims=True))
    return jnp.where(flags[...] > 0, wanted - jnp.concatenate(interpolated, axis=0), 0.0)


def depth_cells(bricks):
    first = 4 * lax.rem(bricks, 64)
    wanted = jnp.concatenate([first + k for k in range(4)], axis=1)
    z = lax.broadcasted_iota(jnp.int32, (256, 512), 0)
    return jnp.where(z == wanted, 1.0, 0.0).astype(jnp.bfloat16)


def spread(impulse, weights, selector):
    terms = jnp.concatenate(
        [
            jnp.concatenate([weights[k] * impulse[c : c + 1] for k in range(4)], axis=1)
            for c in range(3)
        ],
        axis=0,
    )
    top, rest = halves(terms)
    return dot_across(top, selector) + dot_across(rest, selector)


def place_of(px, xi):
    return 2 * xi + 1 - px


def put(padded, start, size, values, stride=None):
    padded[0, pl.ds(start, size, stride)] = values[:, :128]
    padded[1, pl.ds(start, size, stride)] = values[:, 128:]


def take(padded, start, size, stride=None):
    return jnp.concatenate(
        [padded[half, pl.ds(start, size, stride)] for half in range(2)], axis=1
    )


def step_kernel(
    velocity,
    bricks_hbm,
    flags_hbm,
    weights_hbm,
    target_hbm,
    contact_hbm,
    cells_hbm,
    depth_hbm,
    depth_back_hbm,
    rows_hbm,
    rows_back_hbm,
    columns_hbm,
    columns_back_hbm,
    symbol_xz_hbm,
    symbol_y_hbm,
    velocity_new,
    potential,
    impulse_out,
    bricks,
    flags,
    target_velocity,
    contact_force,
    cells,
    symbol_xz,
    symbol_y,
    depth,
    depth_back,
    rows,
    rows_back,
    columns,
    columns_back,
    region,
    weights,
    weights_below,
    bricks_below,
    flags_below,
    target_below,
    contact_below,
    star,
    forced,
    padded,
    classes,
    line_out,
    line_in,
    y_out,
    x_in,
    x_out,
    y_in,
    line_back,
    line_home,
    table_sem,
    near_send,
    near_recv,
    own_sem,
    send_sem,
    recv_sem,
):
    s = lax.axis_index("gx")
    t = lax.axis_index("gy")
    px = t // 4
    py = lax.rem(t // 2, 2)
    loads = [
        pltpu.make_async_copy(source, target, table_sem.at[number])
        for number, (source, target) in enumerate(
            (
                (depth_hbm, depth),
                (depth_back_hbm, depth_back),
                (rows_hbm.at[py], rows),
                (rows_back_hbm.at[py], rows_back),
                (columns_hbm.at[px], columns),
                (columns_back_hbm.at[px], columns_back),
                (velocity, region.at[:, pl.ds(5, 4), pl.ds(8, 16)]),
                (weights_hbm, weights),
                (bricks_hbm, bricks),
                (flags_hbm, flags),
                (target_hbm, target_velocity),
                (contact_hbm, contact_force),
                (cells_hbm, cells),
                (symbol_xz_hbm, symbol_xz),
                (symbol_y_hbm.at[pl.ds(s, 1)], symbol_y),
            )
        )
    ]
    for number in (8, 9, 12, 7, 6, 10, 11, 0, 2, 4, 5, 13, 14, 3, 1):
        loads[number].start()
    line_in[...] = jnp.zeros_like(line_in)
    barrier = pltpu.get_barrier_semaphore()

    def away(dx, dy):
        return (lax.rem(s + GX + dx, GX), lax.rem(t + GY + dy, GY))

    def greet_gx(step, carry):
        pl.semaphore_signal(
            barrier, inc=1, device_id=(lax.rem(s + step, GX), t), device_id_type=MESH
        )
        return carry

    def greet_gy(step, carry):
        pl.semaphore_signal(
            barrier, inc=1, device_id=(s, lax.rem(t + step, GY)), device_id_type=MESH
        )
        return carry

    for dx in (-1, 1):
        for dy in (-1, 1):
            pl.semaphore_signal(barrier, inc=1, device_id=away(dx, dy), device_id_type=MESH)
    lax.fori_loop(1, GY, greet_gy, 0)
    lax.fori_loop(1, GX, greet_gx, 0)
    pl.semaphore_wait(barrier, GX - 1 + GY - 1 + 4)

    near = [
        pltpu.make_async_remote_copy(
            src_ref=source,
            dst_ref=target,
            send_sem=near_send.at[number],
            recv_sem=near_recv.at[number],
            device_id=away(*where),
            device_id_type=MESH,
        )
        for number, (source, target, where) in enumerate(
            (
                (velocity.at[:, :, pl.ds(0, 1)], region.at[:, pl.ds(5, 4), pl.ds(24, 1)], (0, -1)),
                (velocity.at[:, :, pl.ds(0, 1)], region.at[:, pl.ds(9, 4), pl.ds(24, 1)], (-1, -1)),
                (velocity.at[:, :, pl.ds(0, 1)], region.at[:, pl.ds(1, 4), pl.ds(24, 1)], (1, -1)),
                (velocity.at[:, :, pl.ds(15, 1)], region.at[:, pl.ds(5, 4), pl.ds(7, 1)], (0, 1)),
                (velocity.at[:, :, pl.ds(15, 1)], region.at[:, pl.ds(9, 4), pl.ds(7, 1)], (-1, 1)),
                (velocity.at[:, :, pl.ds(15, 1)], region.at[:, pl.ds(1, 4), pl.ds(7, 1)], (1, 1)),
                (velocity.at[:, pl.ds(0, 1)], region.at[:, pl.ds(13, 1), pl.ds(8, 16)], (-2, 0)),
                (velocity.at[:, pl.ds(3, 1)], region.at[:, pl.ds(0, 1), pl.ds(8, 16)], (2, 0)),
                (bricks_hbm, bricks_below, (1, 0)),
                (flags_hbm, flags_below, (1, 0)),
                (target_hbm, target_below, (1, 0)),
                (contact_hbm, contact_below, (1, 0)),
                (weights_hbm, weights_below, (1, 0)),
                (velocity, region.at[:, pl.ds(9, 4), pl.ds(8, 16)], (-1, 0)),
                (velocity, region.at[:, pl.ds(1, 4), pl.ds(8, 16)], (1, 0)),
            )
        )
    ]
    for copy in near:
        copy.start()

    for number in (8, 9, 12, 7):
        loads[number].wait()
    own_weights, next_weights = both_weights(cells, weights, bricks, flags)
    selector = depth_cells(bricks[...])
    for number in (8, 9, 12):
        near[number].wait_recv()
    below_weights, here_weights = both_weights(cells, weights_below, bricks_below, flags_below)
    selector_below = depth_cells(bricks_below[...])
    for number in (6, 10, 11):
        loads[number].wait()
    for number in (0, 1, 2, 3, 4, 5, 6, 7, 10, 11, 13, 14):
        near[number].wait_recv()
    for x in range(1, 13):
        block, inner = (x - 1) // 4, (x - 1) % 4
        centers = [region[c, x, 8:24] for c in range(3)]
        for c in range(3):
            v = centers[c]
            uppers = (region[c, x + 1, 8:24], region[c, x, 9:25], pltpu.roll(v, 255, 1))
            lowers = (region[c, x - 1, 8:24], region[c, x, 7:23], pltpu.roll(v, 1, 1))
            laplace = -6.0 * v
            carried = jnp.zeros_like(v)
            for d in range(3):
                laplace = laplace + (uppers[d] + lowers[d])
                carried = carried + centers[d] * (uppers[d] - lowers[d])
            base = 192 * block + 64 * c + 16 * inner
            star[base : base + 16] = v + time_step * (viscosity * laplace - 0.5 * carried)

    impulse = impulse_of(
        star[192:576],
        selector,
        (own_weights, next_weights),
        target_velocity[...] + time_step * contact_force[...],
        flags,
    )
    impulse_out[...] = impulse
    impulse_below = impulse_of(
        star[0:384],
        selector_below,
        (below_weights, here_weights),
        target_below[...] + time_step * contact_below[...],
        flags_below,
    )
    at_home = spread(impulse, own_weights, selector)
    from_below = spread(impulse_below, here_weights, selector_below)
    for c in range(3):
        for x in range(4):
            base = 64 * c + 16 * x
            forced[c, x] = star[192 + base : 208 + base] + volume_ratio * (
                at_home[base : base + 16] + from_below[base : base + 16]
            )

    classes[...] = jnp.zeros_like(classes)
    row_number = lax.broadcasted_iota(jnp.int32, (16, 256), 0)
    for place in range(6):
        x = place - 1
        total = jnp.zeros((16, 256), jnp.float32)
        if 0 <= x + 1 < 4:
            total = total + forced[0, x + 1]
        if 0 <= x - 1 < 4:
            total = total - forced[0, x - 1]
        if 0 <= x < 4:
            v = forced[1, x]
            w = forced[2, x]
            upper = jnp.where(row_number == 15, 0.0, pltpu.roll(v, 15, 0))
            lower = jnp.where(row_number == 0, 0.0, pltpu.roll(v, 1, 0))
            total = total + (upper - lower)
            total = total + (pltpu.roll(w, 255, 1) - pltpu.roll(w, 1, 1))
            put(padded, 32 * place + 7, 1, 0.5 * forced[1, x, 0:1])
            put(padded, 32 * place + 24, 1, -0.5 * forced[1, x, 15:16])
        else:
            put(padded, 32 * place + 7, 1, jnp.zeros((1, 256), jnp.float32))
            put(padded, 32 * place + 24, 1, jnp.zeros((1, 256), jnp.float32))
        put(padded, 32 * place + 8, 16, 0.5 * total)
    for a in range(2):
        for b in range(2):
            base = 32 * (2 * a + b)
            for xi in range(3):
                place = 32 * place_of(a, xi)
                classes[base + 8 * xi : base + 8 * xi + 8] = take(padded, place + 8 + b, 8, 2)
                edge = place + (7 if b else 24)
                classes[base + 24 + xi : base + 25 + xi] = take(padded, edge, 1)
    loads[0].wait()
    spectrum = times_table(classes[...], depth)
    for c in range(8):
        line_out[32 * c : 32 * c + 32] = spectrum[
            32 * (c // 2) : 32 * (c // 2) + 32, 128 * (c % 2) : 128 * (c % 2) + 128
        ]
    exchange_gy(s, t, line_out, line_in, own_sem.at[0], send_sem.at[0], recv_sem.at[0])

    loads[2].wait()
    y_out[...] = table_times(rows, line_in[...])
    exchange_gx(s, t, y_out, x_in, own_sem.at[1], send_sem.at[1], recv_sem.at[1])

    for number in (4, 5, 13, 14):
        loads[number].wait()
    symbol = symbol_xz[...] + symbol_y[...]
    positive = symbol > 0
    factor = jnp.where(positive, -1.0 / jnp.where(positive, symbol, 1.0), 0.0)
    x_out[...] = table_times(columns_back, table_times(columns, x_in[...]) * factor)
    exchange_gx(s, t, x_out, y_in, own_sem.at[2], send_sem.at[2], recv_sem.at[2])

    loads[3].wait()
    line_back[...] = table_times(rows_back, y_in[...])
    exchange_gy(s, t, line_back, line_home, own_sem.at[3], send_sem.at[3], recv_sem.at[3])

    loads[1].wait()
    home = jnp.concatenate(
        [
            jnp.concatenate(
                [line_home[64 * c : 64 * c + 32], line_home[64 * c + 32 : 64 * c + 64]], axis=1
            )
            for c in range(4)
        ],
        axis=0,
    )
    classes[...] = times_table(home, depth_back)
    for a in range(2):
        for b in range(2):
            base = 32 * (2 * a + b)
            for xi in range(3):
                place = 32 * place_of(a, xi)
                put(padded, place + 8 + b, 8, classes[base + 8 * xi : base + 8 * xi + 8], 2)
                edge = place + (7 if b else 24)
                put(padded, edge, 1, classes[base + 24 + xi : base + 25 + xi])
    for x in range(4):
        base = 32 * (x + 1)
        p = take(padded, base + 8, 16)
        potential[x] = p
        velocity_new[0, x] = forced[0, x] - 0.5 * (
            take(padded, base + 40, 16) - take(padded, base - 24, 16)
        )
        velocity_new[1, x] = forced[1, x] - 0.5 * (
            take(padded, base + 9, 16) - take(padded, base + 7, 16)
        )
        velocity_new[2, x] = forced[2, x] - 0.5 * (pltpu.roll(p, 255, 1) - pltpu.roll(p, 1, 1))
    for copy in near:
        copy.wait_send()


def step(velocity, owner_brick, particle_flags, weights, target_velocity, contact_force):
    tables = build_tables()
    inside = pl.BlockSpec(memory_space=pltpu.VMEM)
    outside = pl.BlockSpec(memory_space=pltpu.HBM)
    f32, bf16 = jnp.float32, jnp.bfloat16
    return pl.pallas_call(
        step_kernel,
        out_shape=(
            jax.ShapeDtypeStruct((3, 4, 16, 256), f32),
            jax.ShapeDtypeStruct((4, 16, 256), f32),
            jax.ShapeDtypeStruct((3, 128), f32),
        ),
        in_specs=[outside] * 15,
        out_specs=(inside, inside, inside),
        scratch_shapes=[
            pltpu.VMEM((1, 128), jnp.int32),
            pltpu.VMEM((1, 128), jnp.int32),
            pltpu.VMEM((3, 128), f32),
            pltpu.VMEM((3, 128), f32),
            pltpu.VMEM((512, 128), bf16),
            pltpu.VMEM((128, 128), f32),
            pltpu.VMEM((1, 128), f32),
            pltpu.VMEM((2, 256, 256), bf16),
            pltpu.VMEM((2, 256, 256), bf16),
            pltpu.VMEM((2, 192, 256), bf16),
            pltpu.VMEM((2, 256, 192), bf16),
            pltpu.VMEM((2, 128, 192), bf16),
            pltpu.VMEM((2, 192, 128), bf16),
            pltpu.VMEM((3, 14, 32, 256), f32),
            pltpu.VMEM((128, 128), f32),
            pltpu.VMEM((128, 128), f32),
            pltpu.VMEM((1, 128), jnp.int32),
            pltpu.VMEM((1, 128), jnp.int32),
            pltpu.VMEM((3, 128), f32),
            pltpu.VMEM((3, 128), f32),
            pltpu.VMEM((576, 256), f32),
            pltpu.VMEM((3, 4, 16, 256), f32),
            pltpu.VMEM((2, 192, 128), f32),
            pltpu.VMEM((128, 256), f32),
            pltpu.VMEM((256, 128), f32),
            pltpu.VMEM((256, 128), f32),
            pltpu.VMEM((192, 128), f32),
            pltpu.VMEM((192, 128), f32),
            pltpu.VMEM((192, 128), f32),
            pltpu.VMEM((192, 128), f32),
            pltpu.VMEM((256, 128), f32),
            pltpu.VMEM((256, 128), f32),
            pltpu.SemaphoreType.DMA((15,)),
            pltpu.SemaphoreType.DMA((15,)),
            pltpu.SemaphoreType.DMA((15,)),
            pltpu.SemaphoreType.DMA((4,)),
            pltpu.SemaphoreType.DMA((4,)),
            pltpu.SemaphoreType.DMA((4,)),
        ],
        compiler_params=pltpu.CompilerParams(
            collective_id=0, has_side_effects=True, vmem_limit_bytes=60 * 1024 * 1024
        ),
    )(
        velocity,
        owner_brick.reshape(1, 128),
        particle_flags.reshape(1, 128),
        weights,
        target_velocity,
        contact_force,
        *[jnp.asarray(table) for table in tables],
    )


def solution(mesh):
    placed = (
        P(None, "gx", "gy", None),
        P(("gx", "gy")),
        P(("gx", "gy")),
        P(("gx", "gy"), None),
        P(None, ("gx", "gy")),
        P(None, ("gx", "gy")),
    )
    return jax.shard_map(
        step,
        mesh=mesh,
        in_specs=placed,
        out_specs=(P(None, "gx", "gy", None), P("gx", "gy", None), P(None, ("gx", "gy"))),
        check_vma=False,
    )
```

```python
import jax
import jax.numpy as jnp
import ml_dtypes
import numpy as np
from jax import lax
from jax.experimental import pallas as pl
from jax.experimental.pallas import tpu as pltpu
from jax.sharding import PartitionSpec as P

time_step = 0.05
viscosity = 2.0
volume_ratio = 16.0

MESH = pl.DeviceIdType.MESH
GX, GY = 64, 8


def cas_table(points):
    index = np.arange(points)
    angle = 2.0 * np.pi * (np.outer(index, index) % points) / points
    return (np.cos(angle) + np.sin(angle)) / np.sqrt(points)


def in_two(table):
    top = table.astype(np.float32).astype(ml_dtypes.bfloat16)
    rest = (table - top.astype(np.float64)).astype(ml_dtypes.bfloat16)
    return np.stack([top, rest])


def build_tables():
    cas_128, cas_64 = cas_table(128), cas_table(64)
    depth = np.zeros((256, 256))
    for pz in range(2):
        depth[pz::2, pz * 128 : pz * 128 + 128] = cas_128
    rows = np.zeros((2, 64, 3, 8, 32))
    for py in range(2):
        for t in range(8):
            edge = (8 * t - 1) % 64 if py else (8 * t + 8) % 64
            for xi in range(3):
                rows[py, :, xi, t, 8 * xi : 8 * xi + 8] = cas_64[:, 8 * t : 8 * t + 8]
                rows[py, :, xi, t, 24 + xi] = cas_64[:, edge]
    rows = rows.reshape(2, 192, 256)
    columns = np.zeros((2, 128, 64, 3))
    for px in range(2):
        for xi in range(3):
            columns[px, :, :, xi] = cas_128[:, (2 * np.arange(64) + xi - px) % 128]
    columns = columns.reshape(2, 128, 192)

    n, kk, i, y = np.indices((2, 4, 4, 16)).reshape(4, 512)
    cells = np.arange(128) == (64 * n + 16 * i + 4 * (y % 4) + kk)[:, None]

    def both(tables):
        return np.stack([in_two(table) for table in tables])

    square_128 = np.sin(np.pi * np.arange(128) / 128) ** 2
    square_64 = np.sin(np.pi * np.arange(64) / 64) ** 2
    symbol_xz = (square_128[:, None] + square_128[None, :]).astype(np.float32)
    symbol_y = np.broadcast_to(square_64[:, None], (64, 128)).astype(np.float32)
    return (
        cells.astype(ml_dtypes.bfloat16),
        in_two(depth),
        in_two(depth.T),
        both(rows),
        both(rows.transpose(0, 2, 1)),
        both(columns),
        both(columns.transpose(0, 2, 1)),
        symbol_xz,
        symbol_y,
    )


def halves(values):
    top = values.astype(jnp.bfloat16)
    rest = (values - top.astype(jnp.float32)).astype(jnp.bfloat16)
    return top, rest


def dot(left, right):
    return jnp.dot(left, right, preferred_element_type=jnp.float32)


def table_times(table, values):
    top, rest = halves(values)
    return dot(table[0], top) + (dot(table[1], top) + dot(table[0], rest))


def times_table(values, table):
    top, rest = halves(values)
    return dot(top, table[0]) + (dot(rest, table[0]) + dot(top, table[1]))


def outward(step, size):
    odd = lax.rem(step, 2)
    return size // 2 + (1 - odd) * (step // 2) - odd * ((step + 1) // 2)


def exchange_gx(s, t, source, target, own_sem, send_sem, recv_sem):
    own = pltpu.make_async_copy(source.at[pl.ds(3 * s, 3)], target.at[pl.ds(3 * s, 3)], own_sem)
    own.start()

    def send(step, carry):
        z = lax.rem(s // 8 + outward(step // 8, 8), 8)
        x = lax.rem(lax.rem(s // 2, 4) + outward(lax.rem(step // 2, 4), 4), 4)
        peer = 8 * z + 2 * x + lax.rem(s + 1 + step, 2)
        pltpu.make_async_remote_copy(
            src_ref=source.at[pl.ds(3 * peer, 3)],
            dst_ref=target.at[pl.ds(3 * s, 3)],
            send_sem=send_sem,
            recv_sem=recv_sem,
            device_id=(peer, t),
            device_id_type=MESH,
        ).start()
        return carry

    lax.fori_loop(0, GX - 1, send, 0)
    own.wait()
    moved = pl.ds(0, 3 * (GX - 1))
    pltpu.make_async_copy(source.at[moved], target.at[moved], recv_sem).wait()
    pltpu.make_async_copy(source.at[moved], target.at[moved], send_sem).wait()


def exchange_gy(s, t, source, target, own_sem, send_sem, recv_sem):
    own = pltpu.make_async_copy(source.at[pl.ds(32 * t, 32)], target.at[pl.ds(32 * t, 32)], own_sem)
    own.start()

    def send(step, carry):
        peer = lax.rem(t + outward(step, GY), GY)
        pltpu.make_async_remote_copy(
            src_ref=source.at[pl.ds(32 * peer, 27)],
            dst_ref=target.at[pl.ds(32 * t, 27)],
            send_sem=send_sem,
            recv_sem=recv_sem,
            device_id=(s, peer),
            device_id_type=MESH,
        ).start()
        return carry

    lax.fori_loop(0, GY - 1, send, 0)
    own.wait()
    moved = pl.ds(0, 27 * (GY - 1))
    pltpu.make_async_copy(source.at[moved], target.at[moved], recv_sem).wait()
    pltpu.make_async_copy(source.at[moved], target.at[moved], send_sem).wait()


def dot_across(left, right):
    return lax.dot_general(
        left, right, (((1,), (1,)), ((), ())), preferred_element_type=jnp.float32
    )


def spread_weights(cells, weights, bricks, shown):
    top, rest = halves(weights)
    found = dot_across(cells, top) + dot_across(cells, rest)
    row = lax.broadcasted_iota(jnp.int32, (64, 128), 0)
    mask = (lax.rem(row, 16) // 4 == bricks // 64) & shown
    return [jnp.where(mask, found[64 * k : 64 * k + 64], 0.0) for k in range(4)]


def both_weights(cells, weights, bricks, flags):
    parts = ((cells[0:256], flags[...] > 0), (cells[256:512], flags[...] == 2))
    return [spread_weights(part, weights[...], bricks[...], shown) for part, shown in parts]


def impulse_of(star, selector, weights, wanted, flags):
    top, rest = halves(star)
    found = dot(top, selector) + dot(rest, selector)
    interpolated = []
    for c in range(3):
        total = jnp.zeros((64, 128), jnp.float32)
        for block in range(2):
            base = 192 * block + 64 * c
            for k in range(4):
                cell = found[base : base + 64, 128 * k : 128 * k + 128]
                total = total + cell * weights[block][k]
        interpolated.append(jnp.sum(total, axis=0, keepdims=True))
    return jnp.where(flags[...] > 0, wanted - jnp.concatenate(interpolated, axis=0), 0.0)


def depth_cells(bricks):
    first = 4 * lax.rem(bricks, 64)
    wanted = jnp.concatenate([first + k for k in range(4)], axis=1)
    z = lax.broadcasted_iota(jnp.int32, (256, 512), 0)
    return jnp.where(z == wanted, 1.0, 0.0).astype(jnp.bfloat16)


def spread(impulse, weights, selector):
    terms = jnp.concatenate(
        [
            jnp.concatenate([weights[k] * impulse[c : c + 1] for k in range(4)], axis=1)
            for c in range(3)
        ],
        axis=0,
    )
    top, rest = halves(terms)
    return dot_across(top, selector) + dot_across(rest, selector)


def place_of(px, xi):
    return 2 * xi + 1 - px


def put(padded, start, size, values, stride=None):
    padded[0, pl.ds(start, size, stride)] = values[:, :128]
    padded[1, pl.ds(start, size, stride)] = values[:, 128:]


def take(padded, start, size, stride=None):
    return jnp.concatenate(
        [padded[half, pl.ds(start, size, stride)] for half in range(2)], axis=1
    )


def step_kernel(
    velocity,
    bricks_hbm,
    flags_hbm,
    weights_hbm,
    target_hbm,
    contact_hbm,
    cells_hbm,
    depth_hbm,
    rows_hbm,
    rows_back_hbm,
    columns_hbm,
    columns_back_hbm,
    symbol_xz_hbm,
    symbol_y_hbm,
    forced_out,
    home_out,
    impulse_out,
    bricks,
    flags,
    target_velocity,
    contact_force,
    cells,
    symbol_xz,
    symbol_y,
    depth,
    rows,
    rows_back,
    columns,
    columns_back,
    region,
    weights,
    weights_below,
    bricks_below,
    flags_below,
    target_below,
    contact_below,
    star,
    impulse_kept,
    forced,
    padded,
    classes,
    line_out,
    line_in,
    y_out,
    x_in,
    x_out,
    y_in,
    line_back,
    line_home,
    table_sem,
    near_send,
    near_recv,
    own_sem,
    send_sem,
    recv_sem,
    save_sem,
):
    s = lax.axis_index("gx")
    t = lax.axis_index("gy")
    px = t // 4
    py = lax.rem(t // 2, 2)
    loads = [
        pltpu.make_async_copy(source, target, table_sem.at[number])
        for number, (source, target) in enumerate(
            (
                (depth_hbm, depth),
                (rows_hbm.at[py], rows),
                (rows_back_hbm.at[py], rows_back),
                (columns_hbm.at[px], columns),
                (columns_back_hbm.at[px], columns_back),
                (velocity, region.at[:, pl.ds(5, 4), pl.ds(8, 16)]),
                (weights_hbm, weights),
                (bricks_hbm, bricks),
                (flags_hbm, flags),
                (target_hbm, target_velocity),
                (contact_hbm, contact_force),
                (cells_hbm, cells),
                (symbol_xz_hbm, symbol_xz),
                (symbol_y_hbm.at[pl.ds(s, 1)], symbol_y),
            )
        )
    ]
    for number in (7, 8, 11, 6, 5, 9, 10, 0, 1, 3, 4, 12, 13, 2):
        loads[number].start()
    line_in[...] = jnp.zeros_like(line_in)
    barrier = pltpu.get_barrier_semaphore()

    def away(dx, dy):
        return (lax.rem(s + GX + dx, GX), lax.rem(t + GY + dy, GY))

    def greet_gx(step, carry):
        pl.semaphore_signal(
            barrier, inc=1, device_id=(lax.rem(s + step, GX), t), device_id_type=MESH
        )
        return carry

    def greet_gy(step, carry):
        pl.semaphore_signal(
            barrier, inc=1, device_id=(s, lax.rem(t + step, GY)), device_id_type=MESH
        )
        return carry

    for dx in (-1, 1):
        for dy in (-1, 1):
            pl.semaphore_signal(barrier, inc=1, device_id=away(dx, dy), device_id_type=MESH)
    lax.fori_loop(1, GY, greet_gy, 0)
    lax.fori_loop(1, GX, greet_gx, 0)
    pl.semaphore_wait(barrier, GX - 1 + GY - 1 + 4)

    near = [
        pltpu.make_async_remote_copy(
            src_ref=source,
            dst_ref=target,
            send_sem=near_send.at[number],
            recv_sem=near_recv.at[number],
            device_id=away(*where),
            device_id_type=MESH,
        )
        for number, (source, target, where) in enumerate(
            (
                (velocity.at[:, :, pl.ds(0, 1)], region.at[:, pl.ds(5, 4), pl.ds(24, 1)], (0, -1)),
                (velocity.at[:, :, pl.ds(0, 1)], region.at[:, pl.ds(9, 4), pl.ds(24, 1)], (-1, -1)),
                (velocity.at[:, :, pl.ds(0, 1)], region.at[:, pl.ds(1, 4), pl.ds(24, 1)], (1, -1)),
                (velocity.at[:, :, pl.ds(15, 1)], region.at[:, pl.ds(5, 4), pl.ds(7, 1)], (0, 1)),
                (velocity.at[:, :, pl.ds(15, 1)], region.at[:, pl.ds(9, 4), pl.ds(7, 1)], (-1, 1)),
                (velocity.at[:, :, pl.ds(15, 1)], region.at[:, pl.ds(1, 4), pl.ds(7, 1)], (1, 1)),
                (velocity.at[:, pl.ds(0, 1)], region.at[:, pl.ds(13, 1), pl.ds(8, 16)], (-2, 0)),
                (velocity.at[:, pl.ds(3, 1)], region.at[:, pl.ds(0, 1), pl.ds(8, 16)], (2, 0)),
                (bricks_hbm, bricks_below, (1, 0)),
                (flags_hbm, flags_below, (1, 0)),
                (target_hbm, target_below, (1, 0)),
                (contact_hbm, contact_below, (1, 0)),
                (weights_hbm, weights_below, (1, 0)),
                (velocity, region.at[:, pl.ds(9, 4), pl.ds(8, 16)], (-1, 0)),
                (velocity, region.at[:, pl.ds(1, 4), pl.ds(8, 16)], (1, 0)),
            )
        )
    ]
    for copy in near:
        copy.start()

    for number in (7, 8, 11, 6):
        loads[number].wait()
    own_weights, next_weights = both_weights(cells, weights, bricks, flags)
    selector = depth_cells(bricks[...])
    for number in (8, 9, 12):
        near[number].wait_recv()
    below_weights, here_weights = both_weights(cells, weights_below, bricks_below, flags_below)
    selector_below = depth_cells(bricks_below[...])
    for number in (5, 9, 10):
        loads[number].wait()
    for number in (0, 1, 2, 3, 4, 5, 6, 7, 10, 11, 13, 14):
        near[number].wait_recv()
    for x in range(1, 13):
        block, inner = (x - 1) // 4, (x - 1) % 4
        centers = [region[c, x, 8:24] for c in range(3)]
        for c in range(3):
            v = centers[c]
            uppers = (region[c, x + 1, 8:24], region[c, x, 9:25], pltpu.roll(v, 255, 1))
            lowers = (region[c, x - 1, 8:24], region[c, x, 7:23], pltpu.roll(v, 1, 1))
            laplace = -6.0 * v
            carried = jnp.zeros_like(v)
            for d in range(3):
                laplace = laplace + (uppers[d] + lowers[d])
                carried = carried + centers[d] * (uppers[d] - lowers[d])
            base = 192 * block + 64 * c + 16 * inner
            star[base : base + 16] = v + time_step * (viscosity * laplace - 0.5 * carried)

    impulse = impulse_of(
        star[192:576],
        selector,
        (own_weights, next_weights),
        target_velocity[...] + time_step * contact_force[...],
        flags,
    )
    impulse_kept[...] = impulse
    impulse_below = impulse_of(
        star[0:384],
        selector_below,
        (below_weights, here_weights),
        target_below[...] + time_step * contact_below[...],
        flags_below,
    )
    at_home = spread(impulse, own_weights, selector)
    from_below = spread(impulse_below, here_weights, selector_below)
    for c in range(3):
        for x in range(4):
            base = 64 * c + 16 * x
            forced[c, x] = star[192 + base : 208 + base] + volume_ratio * (
                at_home[base : base + 16] + from_below[base : base + 16]
            )

    saved = [
        pltpu.make_async_copy(impulse_kept, impulse_out, save_sem.at[0]),
        pltpu.make_async_copy(forced, forced_out, save_sem.at[1]),
    ]
    for copy in saved:
        copy.start()

    classes[...] = jnp.zeros_like(classes)
    row_number = lax.broadcasted_iota(jnp.int32, (16, 256), 0)
    for place in range(6):
        x = place - 1
        total = jnp.zeros((16, 256), jnp.float32)
        if 0 <= x + 1 < 4:
            total = total + forced[0, x + 1]
        if 0 <= x - 1 < 4:
            total = total - forced[0, x - 1]
        if 0 <= x < 4:
            v = forced[1, x]
            w = forced[2, x]
            upper = jnp.where(row_number == 15, 0.0, pltpu.roll(v, 15, 0))
            lower = jnp.where(row_number == 0, 0.0, pltpu.roll(v, 1, 0))
            total = total + (upper - lower)
            total = total + (pltpu.roll(w, 255, 1) - pltpu.roll(w, 1, 1))
            put(padded, 32 * place + 7, 1, 0.5 * forced[1, x, 0:1])
            put(padded, 32 * place + 24, 1, -0.5 * forced[1, x, 15:16])
        else:
            put(padded, 32 * place + 7, 1, jnp.zeros((1, 256), jnp.float32))
            put(padded, 32 * place + 24, 1, jnp.zeros((1, 256), jnp.float32))
        put(padded, 32 * place + 8, 16, 0.5 * total)
    for a in range(2):
        for b in range(2):
            base = 32 * (2 * a + b)
            for xi in range(3):
                place = 32 * place_of(a, xi)
                classes[base + 8 * xi : base + 8 * xi + 8] = take(padded, place + 8 + b, 8, 2)
                edge = place + (7 if b else 24)
                classes[base + 24 + xi : base + 25 + xi] = take(padded, edge, 1)
    loads[0].wait()
    spectrum = times_table(classes[...], depth)
    for c in range(8):
        line_out[32 * c : 32 * c + 32] = spectrum[
            32 * (c // 2) : 32 * (c // 2) + 32, 128 * (c % 2) : 128 * (c % 2) + 128
        ]
    exchange_gy(s, t, line_out, line_in, own_sem.at[0], send_sem.at[0], recv_sem.at[0])

    loads[1].wait()
    y_out[...] = table_times(rows, line_in[...])
    exchange_gx(s, t, y_out, x_in, own_sem.at[1], send_sem.at[1], recv_sem.at[1])

    for number in (3, 4, 12, 13):
        loads[number].wait()
    symbol = symbol_xz[...] + symbol_y[...]
    positive = symbol > 0
    factor = jnp.where(positive, -1.0 / jnp.where(positive, symbol, 1.0), 0.0)
    x_out[...] = table_times(columns_back, table_times(columns, x_in[...]) * factor)
    exchange_gx(s, t, x_out, y_in, own_sem.at[2], send_sem.at[2], recv_sem.at[2])

    loads[2].wait()
    line_back[...] = table_times(rows_back, y_in[...])
    exchange_gy(s, t, line_back, line_home, own_sem.at[3], send_sem.at[3], recv_sem.at[3])

    saved.append(pltpu.make_async_copy(line_home, home_out, save_sem.at[2]))
    saved[2].start()
    for copy in saved:
        copy.wait()
    for copy in near:
        copy.wait_send()


def finish_kernel(
    home_hbm,
    depth_back_hbm,
    forced_hbm,
    impulse_hbm,
    velocity_out,
    potential_out,
    impulse_out,
    line_home,
    depth_back,
    forced,
    classes,
    padded,
    potential,
    velocity_new,
    load_sem,
    save_sem,
):
    loads = [
        pltpu.make_async_copy(source, target, load_sem.at[number])
        for number, (source, target) in enumerate(
            ((home_hbm, line_home), (depth_back_hbm, depth_back), (forced_hbm, forced))
        )
    ]
    for load in loads:
        load.start()
    saves = [
        pltpu.make_async_copy(source, target, save_sem.at[number])
        for number, (source, target) in enumerate(
            (
                (impulse_hbm, impulse_out),
                (potential, potential_out),
                (velocity_new.at[0], velocity_out.at[0]),
                (velocity_new.at[1], velocity_out.at[1]),
                (velocity_new.at[2], velocity_out.at[2]),
            )
        )
    ]
    saves[0].start()
    loads[0].wait()
    loads[1].wait()
    home = jnp.concatenate(
        [
            jnp.concatenate(
                [line_home[64 * c : 64 * c + 32], line_home[64 * c + 32 : 64 * c + 64]], axis=1
            )
            for c in range(4)
        ],
        axis=0,
    )
    classes[...] = times_table(home, depth_back)
    for a in range(2):
        for b in range(2):
            base = 32 * (2 * a + b)
            for xi in range(3):
                place = 32 * place_of(a, xi)
                put(padded, place + 8 + b, 8, classes[base + 8 * xi : base + 8 * xi + 8], 2)
                edge = place + (7 if b else 24)
                put(padded, edge, 1, classes[base + 24 + xi : base + 25 + xi])
    for x in range(4):
        potential[x] = take(padded, 32 * x + 40, 16)
    saves[1].start()
    loads[2].wait()
    for x in range(4):
        base = 32 * (x + 1)
        velocity_new[0, x] = forced[0, x] - 0.5 * (
            take(padded, base + 40, 16) - take(padded, base - 24, 16)
        )
    saves[2].start()
    for x in range(4):
        base = 32 * (x + 1)
        velocity_new[1, x] = forced[1, x] - 0.5 * (
            take(padded, base + 9, 16) - take(padded, base + 7, 16)
        )
    saves[3].start()
    for x in range(4):
        p = potential[x]
        velocity_new[2, x] = forced[2, x] - 0.5 * (pltpu.roll(p, 255, 1) - pltpu.roll(p, 1, 1))
    saves[4].start()
    for save in saves:
        save.wait()


def step(velocity, owner_brick, particle_flags, weights, target_velocity, contact_force):
    tables = list(build_tables())
    outside = pl.BlockSpec(memory_space=pltpu.HBM)
    f32, bf16 = jnp.float32, jnp.bfloat16
    depth_back = jnp.asarray(tables.pop(2))
    forced, home, impulse = pl.pallas_call(
        step_kernel,
        out_shape=(
            jax.ShapeDtypeStruct((3, 4, 16, 256), f32),
            jax.ShapeDtypeStruct((256, 128), f32),
            jax.ShapeDtypeStruct((3, 128), f32),
        ),
        in_specs=[outside] * 14,
        out_specs=(outside, outside, outside),
        scratch_shapes=[
            pltpu.VMEM((1, 128), jnp.int32),
            pltpu.VMEM((1, 128), jnp.int32),
            pltpu.VMEM((3, 128), f32),
            pltpu.VMEM((3, 128), f32),
            pltpu.VMEM((512, 128), bf16),
            pltpu.VMEM((128, 128), f32),
            pltpu.VMEM((1, 128), f32),
            pltpu.VMEM((2, 256, 256), bf16),
            pltpu.VMEM((2, 192, 256), bf16),
            pltpu.VMEM((2, 256, 192), bf16),
            pltpu.VMEM((2, 128, 192), bf16),
            pltpu.VMEM((2, 192, 128), bf16),
            pltpu.VMEM((3, 14, 32, 256), f32),
            pltpu.VMEM((128, 128), f32),
            pltpu.VMEM((128, 128), f32),
            pltpu.VMEM((1, 128), jnp.int32),
            pltpu.VMEM((1, 128), jnp.int32),
            pltpu.VMEM((3, 128), f32),
            pltpu.VMEM((3, 128), f32),
            pltpu.VMEM((576, 256), f32),
            pltpu.VMEM((3, 128), f32),
            pltpu.VMEM((3, 4, 16, 256), f32),
            pltpu.VMEM((2, 192, 128), f32),
            pltpu.VMEM((128, 256), f32),
            pltpu.VMEM((256, 128), f32),
            pltpu.VMEM((256, 128), f32),
            pltpu.VMEM((192, 128), f32),
            pltpu.VMEM((192, 128), f32),
            pltpu.VMEM((192, 128), f32),
            pltpu.VMEM((192, 128), f32),
            pltpu.VMEM((256, 128), f32),
            pltpu.VMEM((256, 128), f32),
            pltpu.SemaphoreType.DMA((14,)),
            pltpu.SemaphoreType.DMA((15,)),
            pltpu.SemaphoreType.DMA((15,)),
            pltpu.SemaphoreType.DMA((4,)),
            pltpu.SemaphoreType.DMA((4,)),
            pltpu.SemaphoreType.DMA((4,)),
            pltpu.SemaphoreType.DMA((3,)),
        ],
        compiler_params=pltpu.CompilerParams(
            collective_id=0, has_side_effects=True, vmem_limit_bytes=60 * 1024 * 1024
        ),
    )(
        velocity,
        owner_brick.reshape(1, 128),
        particle_flags.reshape(1, 128),
        weights,
        target_velocity,
        contact_force,
        *[jnp.asarray(table) for table in tables],
    )
    return pl.pallas_call(
        finish_kernel,
        out_shape=(
            jax.ShapeDtypeStruct((3, 4, 16, 256), f32),
            jax.ShapeDtypeStruct((4, 16, 256), f32),
            jax.ShapeDtypeStruct((3, 128), f32),
        ),
        in_specs=[outside] * 4,
        out_specs=(outside, outside, outside),
        scratch_shapes=[
            pltpu.VMEM((256, 128), f32),
            pltpu.VMEM((2, 256, 256), bf16),
            pltpu.VMEM((3, 4, 16, 256), f32),
            pltpu.VMEM((128, 256), f32),
            pltpu.VMEM((2, 192, 128), f32),
            pltpu.VMEM((4, 16, 256), f32),
            pltpu.VMEM((3, 4, 16, 256), f32),
            pltpu.SemaphoreType.DMA((3,)),
            pltpu.SemaphoreType.DMA((5,)),
        ],
        compiler_params=pltpu.CompilerParams(vmem_limit_bytes=60 * 1024 * 1024),
    )(home, depth_back, forced, impulse)


def solution(mesh):
    placed = (
        P(None, "gx", "gy", None),
        P(("gx", "gy")),
        P(("gx", "gy")),
        P(("gx", "gy"), None),
        P(None, ("gx", "gy")),
        P(None, ("gx", "gy")),
    )
    return jax.shard_map(
        step,
        mesh=mesh,
        in_specs=placed,
        out_specs=(P(None, "gx", "gy", None), P("gx", "gy", None), P(None, ("gx", "gy"))),
        check_vma=False,
    )
```

```python
import jax
import jax.numpy as jnp
import ml_dtypes
import numpy as np
from jax import lax
from jax.experimental import pallas as pl
from jax.experimental.pallas import tpu as pltpu
from jax.sharding import PartitionSpec as P

time_step = 0.05
viscosity = 2.0
volume_ratio = 16.0

MESH = pl.DeviceIdType.MESH
GX, GY = 64, 8


def cas_table(points):
    index = np.arange(points)
    angle = 2.0 * np.pi * (np.outer(index, index) % points) / points
    return (np.cos(angle) + np.sin(angle)) / np.sqrt(points)


def in_two(table):
    top = table.astype(np.float32).astype(ml_dtypes.bfloat16)
    rest = (table - top.astype(np.float64)).astype(ml_dtypes.bfloat16)
    return np.stack([top, rest])


def build_tables():
    cas_128, cas_64 = cas_table(128), cas_table(64)
    depth = np.zeros((256, 256))
    for pz in range(2):
        depth[pz::2, pz * 128 : pz * 128 + 128] = cas_128
    rows = np.zeros((2, 64, 3, 8, 32))
    for py in range(2):
        for t in range(8):
            edge = (8 * t - 1) % 64 if py else (8 * t + 8) % 64
            for xi in range(3):
                rows[py, :, xi, t, 8 * xi : 8 * xi + 8] = cas_64[:, 8 * t : 8 * t + 8]
                rows[py, :, xi, t, 24 + xi] = cas_64[:, edge]
    rows = rows.reshape(2, 192, 256)
    columns = np.zeros((2, 128, 64, 3))
    for px in range(2):
        for xi in range(3):
            columns[px, :, :, xi] = cas_128[:, (2 * np.arange(64) + xi - px) % 128]
    columns = columns.reshape(2, 128, 192)

    n, kk, i, y = np.indices((2, 4, 4, 16)).reshape(4, 512)
    cells = np.arange(128) == (64 * n + 16 * i + 4 * (y % 4) + kk)[:, None]

    def both(tables):
        return np.stack([in_two(table) for table in tables])

    square_128 = np.sin(np.pi * np.arange(128) / 128) ** 2
    square_64 = np.sin(np.pi * np.arange(64) / 64) ** 2
    symbol_xz = (square_128[:, None] + square_128[None, :]).astype(np.float32)
    symbol_y = np.broadcast_to(square_64[:, None], (64, 128)).astype(np.float32)
    return (
        cells.astype(ml_dtypes.bfloat16),
        in_two(depth),
        in_two(depth.T),
        both(rows),
        both(rows.transpose(0, 2, 1)),
        both(columns),
        both(columns.transpose(0, 2, 1)),
        symbol_xz,
        symbol_y,
    )


def halves(values):
    top = values.astype(jnp.bfloat16)
    rest = (values - top.astype(jnp.float32)).astype(jnp.bfloat16)
    return top, rest


def dot(left, right):
    return jnp.dot(left, right, preferred_element_type=jnp.float32)


def table_times(table, values):
    top, rest = halves(values)
    return dot(table[0], top) + (dot(table[1], top) + dot(table[0], rest))


def times_table(values, table):
    top, rest = halves(values)
    return dot(top, table[0]) + (dot(rest, table[0]) + dot(top, table[1]))


def outward(step, size):
    odd = lax.rem(step, 2)
    return size // 2 + (1 - odd) * (step // 2) - odd * ((step + 1) // 2)


def exchange_gx(s, t, source, target, own_sem, send_sem, recv_sem):
    own = pltpu.make_async_copy(source.at[pl.ds(3 * s, 3)], target.at[pl.ds(3 * s, 3)], own_sem)
    own.start()

    def send(step, carry):
        z = lax.rem(s // 8 + outward(step // 8, 8), 8)
        x = lax.rem(lax.rem(s // 2, 4) + outward(lax.rem(step // 2, 4), 4), 4)
        peer = 8 * z + 2 * x + lax.rem(s + 1 + step, 2)
        pltpu.make_async_remote_copy(
            src_ref=source.at[pl.ds(3 * peer, 3)],
            dst_ref=target.at[pl.ds(3 * s, 3)],
            send_sem=send_sem,
            recv_sem=recv_sem,
            device_id=(peer, t),
            device_id_type=MESH,
        ).start()
        return carry

    lax.fori_loop(0, GX - 1, send, 0)
    own.wait()
    moved = pl.ds(0, 3 * (GX - 1))
    pltpu.make_async_copy(source.at[moved], target.at[moved], recv_sem).wait()
    pltpu.make_async_copy(source.at[moved], target.at[moved], send_sem).wait()


def exchange_gy(s, t, source, target, own_sem, send_sem, recv_sem):
    own = pltpu.make_async_copy(source.at[pl.ds(32 * t, 32)], target.at[pl.ds(32 * t, 32)], own_sem)
    own.start()

    def send(step, carry):
        peer = lax.rem(t + outward(step, GY), GY)
        pltpu.make_async_remote_copy(
            src_ref=source.at[pl.ds(32 * peer, 27)],
            dst_ref=target.at[pl.ds(32 * t, 27)],
            send_sem=send_sem,
            recv_sem=recv_sem,
            device_id=(s, peer),
            device_id_type=MESH,
        ).start()
        return carry

    lax.fori_loop(0, GY - 1, send, 0)
    own.wait()
    moved = pl.ds(0, 27 * (GY - 1))
    pltpu.make_async_copy(source.at[moved], target.at[moved], recv_sem).wait()
    pltpu.make_async_copy(source.at[moved], target.at[moved], send_sem).wait()


def dot_across(left, right):
    return lax.dot_general(
        left, right, (((1,), (1,)), ((), ())), preferred_element_type=jnp.float32
    )


def spread_weights(cells, weights, bricks, shown):
    top, rest = halves(weights)
    found = dot_across(cells, top) + dot_across(cells, rest)
    row = lax.broadcasted_iota(jnp.int32, (64, 128), 0)
    mask = (lax.rem(row, 16) // 4 == bricks // 64) & shown
    return [jnp.where(mask, found[64 * k : 64 * k + 64], 0.0) for k in range(4)]


def part_of(star, selector, weights):
    top, rest = halves(star)
    found = dot(top, selector) + dot(rest, selector)
    sums = []
    for c in range(3):
        total = jnp.zeros((64, 128), jnp.float32)
        for k in range(4):
            cell = found[64 * c : 64 * c + 64, 128 * k : 128 * k + 128]
            total = total + cell * weights[k]
        sums.append(jnp.sum(total, axis=0, keepdims=True))
    return jnp.concatenate(sums, axis=0)


def depth_cells(bricks):
    first = 4 * lax.rem(bricks, 64)
    wanted = jnp.concatenate([first + k for k in range(4)], axis=1)
    z = lax.broadcasted_iota(jnp.int32, (256, 512), 0)
    return jnp.where(z == wanted, 1.0, 0.0).astype(jnp.bfloat16)


def spread(impulse, weights, selector):
    terms = jnp.concatenate(
        [
            jnp.concatenate([weights[k] * impulse[c : c + 1] for k in range(4)], axis=1)
            for c in range(3)
        ],
        axis=0,
    )
    top, rest = halves(terms)
    return dot_across(top, selector) + dot_across(rest, selector)


def place_of(px, xi):
    return 2 * xi + 1 - px


def put(padded, start, size, values, stride=None):
    padded[0, pl.ds(start, size, stride)] = values[:, :128]
    padded[1, pl.ds(start, size, stride)] = values[:, 128:]


def take(padded, start, size, stride=None):
    return jnp.concatenate(
        [padded[half, pl.ds(start, size, stride)] for half in range(2)], axis=1
    )


def step_kernel(
    velocity,
    bricks_hbm,
    flags_hbm,
    weights_hbm,
    target_hbm,
    contact_hbm,
    cells_hbm,
    depth_hbm,
    rows_hbm,
    rows_back_hbm,
    columns_hbm,
    columns_back_hbm,
    symbol_xz_hbm,
    symbol_y_hbm,
    forced_out,
    home_out,
    impulse_out,
    bricks,
    flags,
    target_velocity,
    contact_force,
    cells,
    symbol_xz,
    symbol_y,
    depth,
    rows,
    rows_back,
    columns,
    columns_back,
    region,
    weights,
    weights_below,
    bricks_below,
    flags_below,
    wanted,
    wanted_below,
    part_here,
    part_next,
    star,
    impulse_kept,
    forced,
    padded,
    classes,
    line_out,
    line_in,
    y_out,
    x_in,
    x_out,
    y_in,
    line_back,
    line_home,
    table_sem,
    near_send,
    near_recv,
    own_sem,
    send_sem,
    recv_sem,
    save_sem,
):
    s = lax.axis_index("gx")
    t = lax.axis_index("gy")
    px = t // 4
    py = lax.rem(t // 2, 2)
    loads = [
        pltpu.make_async_copy(source, target, table_sem.at[number])
        for number, (source, target) in enumerate(
            (
                (depth_hbm, depth),
                (rows_hbm.at[py], rows),
                (rows_back_hbm.at[py], rows_back),
                (columns_hbm.at[px], columns),
                (columns_back_hbm.at[px], columns_back),
                (velocity, region.at[:, pl.ds(1, 4), pl.ds(8, 16)]),
                (weights_hbm, weights),
                (bricks_hbm, bricks),
                (flags_hbm, flags),
                (target_hbm, target_velocity),
                (contact_hbm, contact_force),
                (cells_hbm, cells),
                (symbol_xz_hbm, symbol_xz),
                (symbol_y_hbm.at[pl.ds(s, 1)], symbol_y),
            )
        )
    ]
    for number in (7, 8, 11, 6, 5, 9, 10, 0, 1, 3, 4, 12, 13, 2):
        loads[number].start()
    line_in[...] = jnp.zeros_like(line_in)
    barrier = pltpu.get_barrier_semaphore()

    def away(dx, dy):
        return (lax.rem(s + GX + dx, GX), lax.rem(t + GY + dy, GY))

    def greet_gx(step, carry):
        pl.semaphore_signal(
            barrier, inc=1, device_id=(lax.rem(s + step, GX), t), device_id_type=MESH
        )
        return carry

    def greet_gy(step, carry):
        pl.semaphore_signal(
            barrier, inc=1, device_id=(s, lax.rem(t + step, GY)), device_id_type=MESH
        )
        return carry

    lax.fori_loop(1, GY, greet_gy, 0)
    lax.fori_loop(1, GX, greet_gx, 0)
    pl.semaphore_wait(barrier, GX - 1 + GY - 1)

    near = [
        pltpu.make_async_remote_copy(
            src_ref=source,
            dst_ref=target,
            send_sem=near_send.at[number],
            recv_sem=near_recv.at[number],
            device_id=away(*where),
            device_id_type=MESH,
        )
        for number, (source, target, where) in enumerate(
            (
                (velocity.at[:, :, pl.ds(0, 1)], region.at[:, pl.ds(1, 4), pl.ds(24, 1)], (0, -1)),
                (velocity.at[:, :, pl.ds(15, 1)], region.at[:, pl.ds(1, 4), pl.ds(7, 1)], (0, 1)),
                (velocity.at[:, pl.ds(0, 1)], region.at[:, pl.ds(5, 1), pl.ds(8, 16)], (-1, 0)),
                (velocity.at[:, pl.ds(3, 1)], region.at[:, pl.ds(0, 1), pl.ds(8, 16)], (1, 0)),
                (bricks_hbm, bricks_below, (1, 0)),
                (flags_hbm, flags_below, (1, 0)),
                (weights_hbm, weights_below, (1, 0)),
                (wanted, wanted_below, (1, 0)),
                (part_here, part_next, (-1, 0)),
            )
        )
    ]
    for number in range(7):
        near[number].start()

    for number in (7, 8, 11, 6):
        loads[number].wait()
    live = flags[...] > 0
    own_weights = spread_weights(cells[0:256], weights[...], bricks[...], live)
    selector = depth_cells(bricks[...])
    for number in (4, 5, 6):
        near[number].wait_recv()
    here_weights = spread_weights(
        cells[256:512], weights_below[...], bricks_below[...], flags_below[...] == 2
    )
    selector_below = depth_cells(bricks_below[...])
    for number in (5, 9, 10):
        loads[number].wait()
    for number in range(4):
        near[number].wait_recv()
    for x in range(1, 5):
        centers = [region[c, x, 8:24] for c in range(3)]
        for c in range(3):
            v = centers[c]
            uppers = (region[c, x + 1, 8:24], region[c, x, 9:25], pltpu.roll(v, 255, 1))
            lowers = (region[c, x - 1, 8:24], region[c, x, 7:23], pltpu.roll(v, 1, 1))
            laplace = -6.0 * v
            carried = jnp.zeros_like(v)
            for d in range(3):
                laplace = laplace + (uppers[d] + lowers[d])
                carried = carried + centers[d] * (uppers[d] - lowers[d])
            base = 64 * c + 16 * (x - 1)
            star[base : base + 16] = v + time_step * (viscosity * laplace - 0.5 * carried)

    part_here[...] = part_of(star[...], selector_below, here_weights)
    near[8].start()
    wanted[...] = (
        target_velocity[...]
        + time_step * contact_force[...]
        - part_of(star[...], selector, own_weights)
    )
    near[7].start()
    near[7].wait_recv()
    near[8].wait_recv()
    impulse = jnp.where(live, wanted[...] - part_next[...], 0.0)
    impulse_below = jnp.where(flags_below[...] > 0, wanted_below[...] - part_here[...], 0.0)
    impulse_kept[...] = impulse
    at_home = spread(impulse, own_weights, selector)
    from_below = spread(impulse_below, here_weights, selector_below)
    for c in range(3):
        for x in range(4):
            base = 64 * c + 16 * x
            forced[c, x] = star[base : base + 16] + volume_ratio * (
                at_home[base : base + 16] + from_below[base : base + 16]
            )

    saved = [
        pltpu.make_async_copy(impulse_kept, impulse_out, save_sem.at[0]),
        pltpu.make_async_copy(forced, forced_out, save_sem.at[1]),
    ]
    for copy in saved:
        copy.start()

    classes[...] = jnp.zeros_like(classes)
    row_number = lax.broadcasted_iota(jnp.int32, (16, 256), 0)
    for place in range(6):
        x = place - 1
        total = jnp.zeros((16, 256), jnp.float32)
        if 0 <= x + 1 < 4:
            total = total + forced[0, x + 1]
        if 0 <= x - 1 < 4:
            total = total - forced[0, x - 1]
        if 0 <= x < 4:
            v = forced[1, x]
            w = forced[2, x]
            upper = jnp.where(row_number == 15, 0.0, pltpu.roll(v, 15, 0))
            lower = jnp.where(row_number == 0, 0.0, pltpu.roll(v, 1, 0))
            total = total + (upper - lower)
            total = total + (pltpu.roll(w, 255, 1) - pltpu.roll(w, 1, 1))
            put(padded, 32 * place + 7, 1, 0.5 * forced[1, x, 0:1])
            put(padded, 32 * place + 24, 1, -0.5 * forced[1, x, 15:16])
        else:
            put(padded, 32 * place + 7, 1, jnp.zeros((1, 256), jnp.float32))
            put(padded, 32 * place + 24, 1, jnp.zeros((1, 256), jnp.float32))
        put(padded, 32 * place + 8, 16, 0.5 * total)
    for a in range(2):
        for b in range(2):
            base = 32 * (2 * a + b)
            for xi in range(3):
                place = 32 * place_of(a, xi)
                classes[base + 8 * xi : base + 8 * xi + 8] = take(padded, place + 8 + b, 8, 2)
                edge = place + (7 if b else 24)
                classes[base + 24 + xi : base + 25 + xi] = take(padded, edge, 1)
    loads[0].wait()
    spectrum = times_table(classes[...], depth)
    for c in range(8):
        line_out[32 * c : 32 * c + 32] = spectrum[
            32 * (c // 2) : 32 * (c // 2) + 32, 128 * (c % 2) : 128 * (c % 2) + 128
        ]
    exchange_gy(s, t, line_out, line_in, own_sem.at[0], send_sem.at[0], recv_sem.at[0])

    loads[1].wait()
    y_out[...] = table_times(rows, line_in[...])
    exchange_gx(s, t, y_out, x_in, own_sem.at[1], send_sem.at[1], recv_sem.at[1])

    for number in (3, 4, 12, 13):
        loads[number].wait()
    symbol = symbol_xz[...] + symbol_y[...]
    positive = symbol > 0
    factor = jnp.where(positive, -1.0 / jnp.where(positive, symbol, 1.0), 0.0)
    x_out[...] = table_times(columns_back, table_times(columns, x_in[...]) * factor)
    exchange_gx(s, t, x_out, y_in, own_sem.at[2], send_sem.at[2], recv_sem.at[2])

    loads[2].wait()
    line_back[...] = table_times(rows_back, y_in[...])
    exchange_gy(s, t, line_back, line_home, own_sem.at[3], send_sem.at[3], recv_sem.at[3])

    saved.append(pltpu.make_async_copy(line_home, home_out, save_sem.at[2]))
    saved[2].start()
    for copy in saved:
        copy.wait()
    for copy in near:
        copy.wait_send()


def finish_kernel(
    home_hbm,
    depth_back_hbm,
    forced_hbm,
    impulse_hbm,
    velocity_out,
    potential_out,
    impulse_out,
    line_home,
    depth_back,
    forced,
    classes,
    padded,
    potential,
    velocity_new,
    load_sem,
    save_sem,
):
    loads = [
        pltpu.make_async_copy(source, target, load_sem.at[number])
        for number, (source, target) in enumerate(
            ((home_hbm, line_home), (depth_back_hbm, depth_back), (forced_hbm, forced))
        )
    ]
    for load in loads:
        load.start()
    saves = [
        pltpu.make_async_copy(source, target, save_sem.at[number])
        for number, (source, target) in enumerate(
            (
                (impulse_hbm, impulse_out),
                (potential, potential_out),
                (velocity_new.at[0], velocity_out.at[0]),
                (velocity_new.at[1], velocity_out.at[1]),
                (velocity_new.at[2], velocity_out.at[2]),
            )
        )
    ]
    saves[0].start()
    loads[0].wait()
    loads[1].wait()
    home = jnp.concatenate(
        [
            jnp.concatenate(
                [line_home[64 * c : 64 * c + 32], line_home[64 * c + 32 : 64 * c + 64]], axis=1
            )
            for c in range(4)
        ],
        axis=0,
    )
    classes[...] = times_table(home, depth_back)
    for a in range(2):
        for b in range(2):
            base = 32 * (2 * a + b)
            for xi in range(3):
                place = 32 * place_of(a, xi)
                put(padded, place + 8 + b, 8, classes[base + 8 * xi : base + 8 * xi + 8], 2)
                edge = place + (7 if b else 24)
                put(padded, edge, 1, classes[base + 24 + xi : base + 25 + xi])
    for x in range(4):
        potential[x] = take(padded, 32 * x + 40, 16)
    saves[1].start()
    loads[2].wait()
    for x in range(4):
        base = 32 * (x + 1)
        velocity_new[0, x] = forced[0, x] - 0.5 * (
            take(padded, base + 40, 16) - take(padded, base - 24, 16)
        )
    saves[2].start()
    for x in range(4):
        base = 32 * (x + 1)
        velocity_new[1, x] = forced[1, x] - 0.5 * (
            take(padded, base + 9, 16) - take(padded, base + 7, 16)
        )
    saves[3].start()
    for x in range(4):
        p = potential[x]
        velocity_new[2, x] = forced[2, x] - 0.5 * (pltpu.roll(p, 255, 1) - pltpu.roll(p, 1, 1))
    saves[4].start()
    for save in saves:
        save.wait()


def step(velocity, owner_brick, particle_flags, weights, target_velocity, contact_force):
    tables = list(build_tables())
    outside = pl.BlockSpec(memory_space=pltpu.HBM)
    f32, bf16 = jnp.float32, jnp.bfloat16
    depth_back = jnp.asarray(tables.pop(2))
    forced, home, impulse = pl.pallas_call(
        step_kernel,
        out_shape=(
            jax.ShapeDtypeStruct((3, 4, 16, 256), f32),
            jax.ShapeDtypeStruct((256, 128), f32),
            jax.ShapeDtypeStruct((3, 128), f32),
        ),
        in_specs=[outside] * 14,
        out_specs=(outside, outside, outside),
        scratch_shapes=[
            pltpu.VMEM((1, 128), jnp.int32),
            pltpu.VMEM((1, 128), jnp.int32),
            pltpu.VMEM((3, 128), f32),
            pltpu.VMEM((3, 128), f32),
            pltpu.VMEM((512, 128), bf16),
            pltpu.VMEM((128, 128), f32),
            pltpu.VMEM((1, 128), f32),
            pltpu.VMEM((2, 256, 256), bf16),
            pltpu.VMEM((2, 192, 256), bf16),
            pltpu.VMEM((2, 256, 192), bf16),
            pltpu.VMEM((2, 128, 192), bf16),
            pltpu.VMEM((2, 192, 128), bf16),
            pltpu.VMEM((3, 6, 32, 256), f32),
            pltpu.VMEM((128, 128), f32),
            pltpu.VMEM((128, 128), f32),
            pltpu.VMEM((1, 128), jnp.int32),
            pltpu.VMEM((1, 128), jnp.int32),
            pltpu.VMEM((3, 128), f32),
            pltpu.VMEM((3, 128), f32),
            pltpu.VMEM((3, 128), f32),
            pltpu.VMEM((3, 128), f32),
            pltpu.VMEM((192, 256), f32),
            pltpu.VMEM((3, 128), f32),
            pltpu.VMEM((3, 4, 16, 256), f32),
            pltpu.VMEM((2, 192, 128), f32),
            pltpu.VMEM((128, 256), f32),
            pltpu.VMEM((256, 128), f32),
            pltpu.VMEM((256, 128), f32),
            pltpu.VMEM((192, 128), f32),
            pltpu.VMEM((192, 128), f32),
            pltpu.VMEM((192, 128), f32),
            pltpu.VMEM((192, 128), f32),
            pltpu.VMEM((256, 128), f32),
            pltpu.VMEM((256, 128), f32),
            pltpu.SemaphoreType.DMA((14,)),
            pltpu.SemaphoreType.DMA((9,)),
            pltpu.SemaphoreType.DMA((9,)),
            pltpu.SemaphoreType.DMA((4,)),
            pltpu.SemaphoreType.DMA((4,)),
            pltpu.SemaphoreType.DMA((4,)),
            pltpu.SemaphoreType.DMA((3,)),
        ],
        compiler_params=pltpu.CompilerParams(
            collective_id=0, has_side_effects=True, vmem_limit_bytes=60 * 1024 * 1024
        ),
    )(
        velocity,
        owner_brick.reshape(1, 128),
        particle_flags.reshape(1, 128),
        weights,
        target_velocity,
        contact_force,
        *[jnp.asarray(table) for table in tables],
    )
    return pl.pallas_call(
        finish_kernel,
        out_shape=(
            jax.ShapeDtypeStruct((3, 4, 16, 256), f32),
            jax.ShapeDtypeStruct((4, 16, 256), f32),
            jax.ShapeDtypeStruct((3, 128), f32),
        ),
        in_specs=[outside] * 4,
        out_specs=(outside, outside, outside),
        scratch_shapes=[
            pltpu.VMEM((256, 128), f32),
            pltpu.VMEM((2, 256, 256), bf16),
            pltpu.VMEM((3, 4, 16, 256), f32),
            pltpu.VMEM((128, 256), f32),
            pltpu.VMEM((2, 192, 128), f32),
            pltpu.VMEM((4, 16, 256), f32),
            pltpu.VMEM((3, 4, 16, 256), f32),
            pltpu.SemaphoreType.DMA((3,)),
            pltpu.SemaphoreType.DMA((5,)),
        ],
        compiler_params=pltpu.CompilerParams(vmem_limit_bytes=60 * 1024 * 1024),
    )(home, depth_back, forced, impulse)


def solution(mesh):
    placed = (
        P(None, "gx", "gy", None),
        P(("gx", "gy")),
        P(("gx", "gy")),
        P(("gx", "gy"), None),
        P(None, ("gx", "gy")),
        P(None, ("gx", "gy")),
    )
    return jax.shard_map(
        step,
        mesh=mesh,
        in_specs=placed,
        out_specs=(P(None, "gx", "gy", None), P("gx", "gy", None), P(None, ("gx", "gy"))),
        check_vma=False,
    )
```

```python
import jax
import jax.numpy as jnp
import ml_dtypes
import numpy as np
from jax import lax
from jax.experimental import pallas as pl
from jax.experimental.pallas import tpu as pltpu
from jax.sharding import PartitionSpec as P

time_step = 0.05
viscosity = 2.0
volume_ratio = 16.0

MESH = pl.DeviceIdType.MESH
GX, GY = 64, 8


def cas_table(points):
    index = np.arange(points)
    angle = 2.0 * np.pi * (np.outer(index, index) % points) / points
    return (np.cos(angle) + np.sin(angle)) / np.sqrt(points)


def in_two(table):
    top = table.astype(np.float32).astype(ml_dtypes.bfloat16)
    rest = (table - top.astype(np.float64)).astype(ml_dtypes.bfloat16)
    return np.stack([top, rest])


def build_tables():
    cas_128, cas_64 = cas_table(128), cas_table(64)
    depth = np.zeros((256, 256))
    for pz in range(2):
        depth[pz::2, pz * 128 : pz * 128 + 128] = cas_128
    rows = np.zeros((2, 64, 3, 8, 32))
    for py in range(2):
        for t in range(8):
            edge = (8 * t - 1) % 64 if py else (8 * t + 8) % 64
            for xi in range(3):
                rows[py, :, xi, t, 8 * xi : 8 * xi + 8] = cas_64[:, 8 * t : 8 * t + 8]
                rows[py, :, xi, t, 24 + xi] = cas_64[:, edge]
    rows = rows.reshape(2, 192, 256)
    columns = np.zeros((2, 128, 64, 3))
    for px in range(2):
        for xi in range(3):
            columns[px, :, :, xi] = cas_128[:, (2 * np.arange(64) + xi - px) % 128]
    columns = columns.reshape(2, 128, 192)

    n, kk, i, y = np.indices((2, 4, 4, 16)).reshape(4, 512)
    cells = np.arange(128) == (64 * n + 16 * i + 4 * (y % 4) + kk)[:, None]

    def both(tables):
        return np.stack([in_two(table) for table in tables])

    square_128 = np.sin(np.pi * np.arange(128) / 128) ** 2
    square_64 = np.sin(np.pi * np.arange(64) / 64) ** 2
    symbol_xz = (square_128[:, None] + square_128[None, :]).astype(np.float32)
    symbol_y = np.broadcast_to(square_64[:, None], (64, 128)).astype(np.float32)
    return (
        cells.astype(ml_dtypes.bfloat16),
        in_two(depth),
        in_two(depth.T),
        both(rows),
        both(rows.transpose(0, 2, 1)),
        both(columns),
        both(columns.transpose(0, 2, 1)),
        symbol_xz,
        symbol_y,
    )


def halves(values):
    top = values.astype(jnp.bfloat16)
    rest = (values - top.astype(jnp.float32)).astype(jnp.bfloat16)
    return top, rest


def dot(left, right):
    return jnp.dot(left, right, preferred_element_type=jnp.float32)


def table_times(table, values):
    top, rest = halves(values)
    return dot(table[0], top) + (dot(table[1], top) + dot(table[0], rest))


def times_table(values, table):
    top, rest = halves(values)
    return dot(top, table[0]) + (dot(rest, table[0]) + dot(top, table[1]))


def outward(step, size):
    odd = lax.rem(step, 2)
    return size // 2 + (1 - odd) * (step // 2) - odd * ((step + 1) // 2)


def exchange_gx(s, t, source, target, own_sem, send_sem, recv_sem):
    own = pltpu.make_async_copy(source.at[pl.ds(3 * s, 3)], target.at[pl.ds(3 * s, 3)], own_sem)
    own.start()

    chip = lax.rem(s // 2, 4)
    beside = [
        2 * lax.rem(chip + dx, 4) + lax.rem(s + dc, 2) for dx in (2, 1, 3, 0) for dc in (1, 0)
    ]

    def send_to(peer):
        pltpu.make_async_remote_copy(
            src_ref=source.at[pl.ds(3 * peer, 3)],
            dst_ref=target.at[pl.ds(3 * s, 3)],
            send_sem=send_sem,
            recv_sem=recv_sem,
            device_id=(peer, t),
            device_id_type=MESH,
        ).start()

    def send(step, carry):
        layer = 8 * lax.rem(s // 8 + outward(step, 8), 8)
        for low in beside:
            send_to(layer + low)
        return carry

    lax.fori_loop(0, 7, send, 0)
    for low in beside[:7]:
        send_to(8 * (s // 8) + low)
    own.wait()
    moved = pl.ds(0, 3 * (GX - 1))
    pltpu.make_async_copy(source.at[moved], target.at[moved], recv_sem).wait()
    pltpu.make_async_copy(source.at[moved], target.at[moved], send_sem).wait()


def exchange_gy(s, t, source, target, own_sem, send_sem, recv_sem):
    own = pltpu.make_async_copy(source.at[pl.ds(32 * t, 32)], target.at[pl.ds(32 * t, 32)], own_sem)
    own.start()

    for dy in (4, 3, 5, 2, 6, 1, 7):
        peer = lax.rem(t + dy, GY)
        pltpu.make_async_remote_copy(
            src_ref=source.at[pl.ds(32 * peer, 27)],
            dst_ref=target.at[pl.ds(32 * t, 27)],
            send_sem=send_sem,
            recv_sem=recv_sem,
            device_id=(s, peer),
            device_id_type=MESH,
        ).start()
    own.wait()
    moved = pl.ds(0, 27 * (GY - 1))
    pltpu.make_async_copy(source.at[moved], target.at[moved], recv_sem).wait()
    pltpu.make_async_copy(source.at[moved], target.at[moved], send_sem).wait()


def dot_across(left, right):
    return lax.dot_general(
        left, right, (((1,), (1,)), ((), ())), preferred_element_type=jnp.float32
    )


def spread_weights(cells, weights, bricks, shown):
    top, rest = halves(weights)
    found = dot_across(cells, top) + dot_across(cells, rest)
    row = lax.broadcasted_iota(jnp.int32, (64, 128), 0)
    mask = (lax.rem(row, 16) // 4 == bricks // 64) & shown
    return [jnp.where(mask, found[64 * k : 64 * k + 64], 0.0) for k in range(4)]


def part_of(star, selector, weights):
    top, rest = halves(star)
    found = dot(top, selector) + dot(rest, selector)
    sums = []
    for c in range(3):
        total = jnp.zeros((64, 128), jnp.float32)
        for k in range(4):
            cell = found[64 * c : 64 * c + 64, 128 * k : 128 * k + 128]
            total = total + cell * weights[k]
        sums.append(jnp.sum(total, axis=0, keepdims=True))
    return jnp.concatenate(sums, axis=0)


def depth_cells(bricks):
    first = 4 * lax.rem(bricks, 64)
    wanted = jnp.concatenate([first + k for k in range(4)], axis=1)
    z = lax.broadcasted_iota(jnp.int32, (256, 512), 0)
    return jnp.where(z == wanted, 1.0, 0.0).astype(jnp.bfloat16)


def spread(impulse, weights, selector):
    terms = jnp.concatenate(
        [
            jnp.concatenate([weights[k] * impulse[c : c + 1] for k in range(4)], axis=1)
            for c in range(3)
        ],
        axis=0,
    )
    top, rest = halves(terms)
    return dot_across(top, selector) + dot_across(rest, selector)


def place_of(px, xi):
    return 2 * xi + 1 - px


def put(padded, start, size, values, stride=None):
    padded[0, pl.ds(start, size, stride)] = values[:, :128]
    padded[1, pl.ds(start, size, stride)] = values[:, 128:]


def take(padded, start, size, stride=None):
    return jnp.concatenate(
        [padded[half, pl.ds(start, size, stride)] for half in range(2)], axis=1
    )


def step_kernel(
    velocity,
    bricks_hbm,
    flags_hbm,
    weights_hbm,
    target_hbm,
    contact_hbm,
    cells_hbm,
    depth_hbm,
    rows_hbm,
    rows_back_hbm,
    columns_hbm,
    columns_back_hbm,
    symbol_xz_hbm,
    symbol_y_hbm,
    forced_out,
    home_out,
    impulse_out,
    bricks,
    flags,
    target_velocity,
    contact_force,
    cells,
    symbol_xz,
    symbol_y,
    depth,
    rows,
    rows_back,
    columns,
    columns_back,
    region,
    weights,
    weights_below,
    bricks_below,
    flags_below,
    wanted,
    wanted_below,
    part_here,
    part_next,
    star,
    impulse_kept,
    forced,
    padded,
    classes,
    line_out,
    line_in,
    y_out,
    x_in,
    x_out,
    y_in,
    line_back,
    line_home,
    table_sem,
    near_send,
    near_recv,
    own_sem,
    send_sem,
    recv_sem,
    save_sem,
):
    s = lax.axis_index("gx")
    t = lax.axis_index("gy")
    px = t // 4
    py = lax.rem(t // 2, 2)
    loads = [
        pltpu.make_async_copy(source, target, table_sem.at[number])
        for number, (source, target) in enumerate(
            (
                (depth_hbm, depth),
                (rows_hbm.at[py], rows),
                (rows_back_hbm.at[py], rows_back),
                (columns_hbm.at[px], columns),
                (columns_back_hbm.at[px], columns_back),
                (velocity, region.at[:, pl.ds(1, 4), pl.ds(8, 16)]),
                (weights_hbm, weights),
                (bricks_hbm, bricks),
                (flags_hbm, flags),
                (target_hbm, target_velocity),
                (contact_hbm, contact_force),
                (cells_hbm, cells),
                (symbol_xz_hbm, symbol_xz),
                (symbol_y_hbm.at[pl.ds(s, 1)], symbol_y),
            )
        )
    ]
    for number in (7, 8, 11, 6, 5, 9, 10, 0, 1, 3, 4, 12, 13, 2):
        loads[number].start()
    line_in[...] = jnp.zeros_like(line_in)
    barrier = pltpu.get_barrier_semaphore()

    def away(dx, dy):
        return (lax.rem(s + GX + dx, GX), lax.rem(t + GY + dy, GY))

    chip = lax.rem(s // 2, 4)
    beside = [
        2 * lax.rem(chip + dx, 4) + lax.rem(s + dc, 2) for dx in (2, 1, 3, 0) for dc in (1, 0)
    ]

    def greet(where):
        pl.semaphore_signal(barrier, inc=1, device_id=where, device_id_type=MESH)

    def greet_layer(step, carry):
        layer = 8 * lax.rem(s // 8 + outward(step, 8), 8)
        for low in beside:
            greet((layer + low, t))
        return carry

    lax.fori_loop(0, 7, greet_layer, 0)
    for low in beside[:7]:
        greet((8 * (s // 8) + low, t))
    for dy in (4, 3, 5, 2, 6, 1, 7):
        greet((s, lax.rem(t + dy, GY)))
    pl.semaphore_wait(barrier, GX - 1 + GY - 1)

    near = [
        pltpu.make_async_remote_copy(
            src_ref=source,
            dst_ref=target,
            send_sem=near_send.at[number],
            recv_sem=near_recv.at[number],
            device_id=away(*where),
            device_id_type=MESH,
        )
        for number, (source, target, where) in enumerate(
            (
                (velocity.at[:, :, pl.ds(0, 1)], region.at[:, pl.ds(1, 4), pl.ds(24, 1)], (0, -1)),
                (velocity.at[:, :, pl.ds(15, 1)], region.at[:, pl.ds(1, 4), pl.ds(7, 1)], (0, 1)),
                (velocity.at[:, pl.ds(0, 1)], region.at[:, pl.ds(5, 1), pl.ds(8, 16)], (-1, 0)),
                (velocity.at[:, pl.ds(3, 1)], region.at[:, pl.ds(0, 1), pl.ds(8, 16)], (1, 0)),
                (bricks_hbm, bricks_below, (1, 0)),
                (flags_hbm, flags_below, (1, 0)),
                (weights_hbm, weights_below, (1, 0)),
                (wanted, wanted_below, (1, 0)),
                (part_here, part_next, (-1, 0)),
            )
        )
    ]
    for number in range(7):
        near[number].start()

    for number in (7, 8, 11, 6):
        loads[number].wait()
    live = flags[...] > 0
    own_weights = spread_weights(cells[0:256], weights[...], bricks[...], live)
    selector = depth_cells(bricks[...])
    for number in (4, 5, 6):
        near[number].wait_recv()
    here_weights = spread_weights(
        cells[256:512], weights_below[...], bricks_below[...], flags_below[...] == 2
    )
    selector_below = depth_cells(bricks_below[...])
    for number in (5, 9, 10):
        loads[number].wait()
    for number in range(4):
        near[number].wait_recv()
    for x in range(1, 5):
        centers = [region[c, x, 8:24] for c in range(3)]
        for c in range(3):
            v = centers[c]
            uppers = (region[c, x + 1, 8:24], region[c, x, 9:25], pltpu.roll(v, 255, 1))
            lowers = (region[c, x - 1, 8:24], region[c, x, 7:23], pltpu.roll(v, 1, 1))
            laplace = -6.0 * v
            carried = jnp.zeros_like(v)
            for d in range(3):
                laplace = laplace + (uppers[d] + lowers[d])
                carried = carried + centers[d] * (uppers[d] - lowers[d])
            base = 64 * c + 16 * (x - 1)
            star[base : base + 16] = v + time_step * (viscosity * laplace - 0.5 * carried)

    part_here[...] = part_of(star[...], selector_below, here_weights)
    near[8].start()
    wanted[...] = (
        target_velocity[...]
        + time_step * contact_force[...]
        - part_of(star[...], selector, own_weights)
    )
    near[7].start()
    near[7].wait_recv()
    near[8].wait_recv()
    impulse = jnp.where(live, wanted[...] - part_next[...], 0.0)
    impulse_below = jnp.where(flags_below[...] > 0, wanted_below[...] - part_here[...], 0.0)
    impulse_kept[...] = impulse
    at_home = spread(impulse, own_weights, selector)
    from_below = spread(impulse_below, here_weights, selector_below)
    for c in range(3):
        for x in range(4):
            base = 64 * c + 16 * x
            forced[c, x] = star[base : base + 16] + volume_ratio * (
                at_home[base : base + 16] + from_below[base : base + 16]
            )

    saved = [
        pltpu.make_async_copy(impulse_kept, impulse_out, save_sem.at[0]),
        pltpu.make_async_copy(forced, forced_out, save_sem.at[1]),
    ]
    for copy in saved:
        copy.start()

    classes[...] = jnp.zeros_like(classes)
    row_number = lax.broadcasted_iota(jnp.int32, (16, 256), 0)
    for place in range(6):
        x = place - 1
        total = jnp.zeros((16, 256), jnp.float32)
        if 0 <= x + 1 < 4:
            total = total + forced[0, x + 1]
        if 0 <= x - 1 < 4:
            total = total - forced[0, x - 1]
        if 0 <= x < 4:
            v = forced[1, x]
            w = forced[2, x]
            upper = jnp.where(row_number == 15, 0.0, pltpu.roll(v, 15, 0))
            lower = jnp.where(row_number == 0, 0.0, pltpu.roll(v, 1, 0))
            total = total + (upper - lower)
            total = total + (pltpu.roll(w, 255, 1) - pltpu.roll(w, 1, 1))
            put(padded, 32 * place + 7, 1, 0.5 * forced[1, x, 0:1])
            put(padded, 32 * place + 24, 1, -0.5 * forced[1, x, 15:16])
        else:
            put(padded, 32 * place + 7, 1, jnp.zeros((1, 256), jnp.float32))
            put(padded, 32 * place + 24, 1, jnp.zeros((1, 256), jnp.float32))
        put(padded, 32 * place + 8, 16, 0.5 * total)
    for a in range(2):
        for b in range(2):
            base = 32 * (2 * a + b)
            for xi in range(3):
                place = 32 * place_of(a, xi)
                classes[base + 8 * xi : base + 8 * xi + 8] = take(padded, place + 8 + b, 8, 2)
                edge = place + (7 if b else 24)
                classes[base + 24 + xi : base + 25 + xi] = take(padded, edge, 1)
    loads[0].wait()
    spectrum = times_table(classes[...], depth)
    for c in range(8):
        line_out[32 * c : 32 * c + 32] = spectrum[
            32 * (c // 2) : 32 * (c // 2) + 32, 128 * (c % 2) : 128 * (c % 2) + 128
        ]
    exchange_gy(s, t, line_out, line_in, own_sem.at[0], send_sem.at[0], recv_sem.at[0])

    loads[1].wait()
    y_out[...] = table_times(rows, line_in[...])
    exchange_gx(s, t, y_out, x_in, own_sem.at[1], send_sem.at[1], recv_sem.at[1])

    for number in (3, 4, 12, 13):
        loads[number].wait()
    symbol = symbol_xz[...] + symbol_y[...]
    positive = symbol > 0
    factor = jnp.where(positive, -1.0 / jnp.where(positive, symbol, 1.0), 0.0)
    x_out[...] = table_times(columns_back, table_times(columns, x_in[...]) * factor)
    exchange_gx(s, t, x_out, y_in, own_sem.at[2], send_sem.at[2], recv_sem.at[2])

    loads[2].wait()
    line_back[...] = table_times(rows_back, y_in[...])
    exchange_gy(s, t, line_back, line_home, own_sem.at[3], send_sem.at[3], recv_sem.at[3])

    saved.append(pltpu.make_async_copy(line_home, home_out, save_sem.at[2]))
    saved[2].start()
    for copy in saved:
        copy.wait()
    for copy in near:
        copy.wait_send()


def finish_kernel(
    home_hbm,
    depth_back_hbm,
    forced_hbm,
    impulse_hbm,
    velocity_out,
    potential_out,
    impulse_out,
    line_home,
    depth_back,
    forced,
    classes,
    padded,
    potential,
    velocity_new,
    load_sem,
    save_sem,
):
    loads = [
        pltpu.make_async_copy(source, target, load_sem.at[number])
        for number, (source, target) in enumerate(
            ((home_hbm, line_home), (depth_back_hbm, depth_back), (forced_hbm, forced))
        )
    ]
    for load in loads:
        load.start()
    saves = [
        pltpu.make_async_copy(source, target, save_sem.at[number])
        for number, (source, target) in enumerate(
            (
                (impulse_hbm, impulse_out),
                (potential, potential_out),
                (velocity_new.at[0], velocity_out.at[0]),
                (velocity_new.at[1], velocity_out.at[1]),
                (velocity_new.at[2], velocity_out.at[2]),
            )
        )
    ]
    saves[0].start()
    loads[0].wait()
    loads[1].wait()
    home = jnp.concatenate(
        [
            jnp.concatenate(
                [line_home[64 * c : 64 * c + 32], line_home[64 * c + 32 : 64 * c + 64]], axis=1
            )
            for c in range(4)
        ],
        axis=0,
    )
    classes[...] = times_table(home, depth_back)
    for a in range(2):
        for b in range(2):
            base = 32 * (2 * a + b)
            for xi in range(3):
                place = 32 * place_of(a, xi)
                put(padded, place + 8 + b, 8, classes[base + 8 * xi : base + 8 * xi + 8], 2)
                edge = place + (7 if b else 24)
                put(padded, edge, 1, classes[base + 24 + xi : base + 25 + xi])
    for x in range(4):
        potential[x] = take(padded, 32 * x + 40, 16)
    saves[1].start()
    loads[2].wait()
    for x in range(4):
        base = 32 * (x + 1)
        velocity_new[0, x] = forced[0, x] - 0.5 * (
            take(padded, base + 40, 16) - take(padded, base - 24, 16)
        )
    saves[2].start()
    for x in range(4):
        base = 32 * (x + 1)
        velocity_new[1, x] = forced[1, x] - 0.5 * (
            take(padded, base + 9, 16) - take(padded, base + 7, 16)
        )
    saves[3].start()
    for x in range(4):
        p = potential[x]
        velocity_new[2, x] = forced[2, x] - 0.5 * (pltpu.roll(p, 255, 1) - pltpu.roll(p, 1, 1))
    saves[4].start()
    for save in saves:
        save.wait()


def step(velocity, owner_brick, particle_flags, weights, target_velocity, contact_force):
    tables = list(build_tables())
    outside = pl.BlockSpec(memory_space=pltpu.HBM)
    f32, bf16 = jnp.float32, jnp.bfloat16
    depth_back = jnp.asarray(tables.pop(2))
    forced, home, impulse = pl.pallas_call(
        step_kernel,
        out_shape=(
            jax.ShapeDtypeStruct((3, 4, 16, 256), f32),
            jax.ShapeDtypeStruct((256, 128), f32),
            jax.ShapeDtypeStruct((3, 128), f32),
        ),
        in_specs=[outside] * 14,
        out_specs=(outside, outside, outside),
        scratch_shapes=[
            pltpu.VMEM((1, 128), jnp.int32),
            pltpu.VMEM((1, 128), jnp.int32),
            pltpu.VMEM((3, 128), f32),
            pltpu.VMEM((3, 128), f32),
            pltpu.VMEM((512, 128), bf16),
            pltpu.VMEM((128, 128), f32),
            pltpu.VMEM((1, 128), f32),
            pltpu.VMEM((2, 256, 256), bf16),
            pltpu.VMEM((2, 192, 256), bf16),
            pltpu.VMEM((2, 256, 192), bf16),
            pltpu.VMEM((2, 128, 192), bf16),
            pltpu.VMEM((2, 192, 128), bf16),
            pltpu.VMEM((3, 6, 32, 256), f32),
            pltpu.VMEM((128, 128), f32),
            pltpu.VMEM((128, 128), f32),
            pltpu.VMEM((1, 128), jnp.int32),
            pltpu.VMEM((1, 128), jnp.int32),
            pltpu.VMEM((3, 128), f32),
            pltpu.VMEM((3, 128), f32),
            pltpu.VMEM((3, 128), f32),
            pltpu.VMEM((3, 128), f32),
            pltpu.VMEM((192, 256), f32),
            pltpu.VMEM((3, 128), f32),
            pltpu.VMEM((3, 4, 16, 256), f32),
            pltpu.VMEM((2, 192, 128), f32),
            pltpu.VMEM((128, 256), f32),
            pltpu.VMEM((256, 128), f32),
            pltpu.VMEM((256, 128), f32),
            pltpu.VMEM((192, 128), f32),
            pltpu.VMEM((192, 128), f32),
            pltpu.VMEM((192, 128), f32),
            pltpu.VMEM((192, 128), f32),
            pltpu.VMEM((256, 128), f32),
            pltpu.VMEM((256, 128), f32),
            pltpu.SemaphoreType.DMA((14,)),
            pltpu.SemaphoreType.DMA((9,)),
            pltpu.SemaphoreType.DMA((9,)),
            pltpu.SemaphoreType.DMA((4,)),
            pltpu.SemaphoreType.DMA((4,)),
            pltpu.SemaphoreType.DMA((4,)),
            pltpu.SemaphoreType.DMA((3,)),
        ],
        compiler_params=pltpu.CompilerParams(
            collective_id=0, has_side_effects=True, vmem_limit_bytes=60 * 1024 * 1024
        ),
    )(
        velocity,
        owner_brick.reshape(1, 128),
        particle_flags.reshape(1, 128),
        weights,
        target_velocity,
        contact_force,
        *[jnp.asarray(table) for table in tables],
    )
    return pl.pallas_call(
        finish_kernel,
        out_shape=(
            jax.ShapeDtypeStruct((3, 4, 16, 256), f32),
            jax.ShapeDtypeStruct((4, 16, 256), f32),
            jax.ShapeDtypeStruct((3, 128), f32),
        ),
        in_specs=[outside] * 4,
        out_specs=(outside, outside, outside),
        scratch_shapes=[
            pltpu.VMEM((256, 128), f32),
            pltpu.VMEM((2, 256, 256), bf16),
            pltpu.VMEM((3, 4, 16, 256), f32),
            pltpu.VMEM((128, 256), f32),
            pltpu.VMEM((2, 192, 128), f32),
            pltpu.VMEM((4, 16, 256), f32),
            pltpu.VMEM((3, 4, 16, 256), f32),
            pltpu.SemaphoreType.DMA((3,)),
            pltpu.SemaphoreType.DMA((5,)),
        ],
        compiler_params=pltpu.CompilerParams(vmem_limit_bytes=60 * 1024 * 1024),
    )(home, depth_back, forced, impulse)


def solution(mesh):
    placed = (
        P(None, "gx", "gy", None),
        P(("gx", "gy")),
        P(("gx", "gy")),
        P(("gx", "gy"), None),
        P(None, ("gx", "gy")),
        P(None, ("gx", "gy")),
    )
    return jax.shard_map(
        step,
        mesh=mesh,
        in_specs=placed,
        out_specs=(P(None, "gx", "gy", None), P("gx", "gy", None), P(None, ("gx", "gy"))),
        check_vma=False,
    )
```

```python
import jax
import jax.numpy as jnp
import ml_dtypes
import numpy as np
from jax import lax
from jax.experimental import pallas as pl
from jax.experimental.pallas import tpu as pltpu
from jax.sharding import PartitionSpec as P

time_step = 0.05
viscosity = 2.0
volume_ratio = 16.0

MESH = pl.DeviceIdType.MESH
GX, GY = 64, 8


def cas_table(points):
    index = np.arange(points)
    angle = 2.0 * np.pi * (np.outer(index, index) % points) / points
    return (np.cos(angle) + np.sin(angle)) / np.sqrt(points)


def in_two(table):
    top = table.astype(np.float32).astype(ml_dtypes.bfloat16)
    rest = (table - top.astype(np.float64)).astype(ml_dtypes.bfloat16)
    return np.stack([top, rest])


def build_tables():
    cas_128, cas_64 = cas_table(128), cas_table(64)
    depth = np.zeros((256, 256))
    for pz in range(2):
        depth[pz::2, pz * 128 : pz * 128 + 128] = cas_128
    rows = np.zeros((2, 64, 3, 8, 32))
    for py in range(2):
        for t in range(8):
            edge = (8 * t - 1) % 64 if py else (8 * t + 8) % 64
            for xi in range(3):
                rows[py, :, xi, t, 8 * xi : 8 * xi + 8] = cas_64[:, 8 * t : 8 * t + 8]
                rows[py, :, xi, t, 24 + xi] = cas_64[:, edge]
    rows = rows.reshape(2, 192, 256)
    columns = np.zeros((2, 128, 64, 3))
    for px in range(2):
        for xi in range(3):
            columns[px, :, :, xi] = cas_128[:, (2 * np.arange(64) + xi - px) % 128]
    columns = columns.reshape(2, 128, 192)

    n, kk, i, y = np.indices((2, 4, 4, 16)).reshape(4, 512)
    cells = np.arange(128) == (64 * n + 16 * i + 4 * (y % 4) + kk)[:, None]

    def both(tables):
        return np.stack([in_two(table) for table in tables])

    square_128 = np.sin(np.pi * np.arange(128) / 128) ** 2
    square_64 = np.sin(np.pi * np.arange(64) / 64) ** 2
    symbol_xz = (square_128[:, None] + square_128[None, :]).astype(np.float32)
    symbol_y = np.broadcast_to(square_64[:, None], (64, 128)).astype(np.float32)
    return (
        cells.astype(ml_dtypes.bfloat16),
        in_two(depth),
        in_two(depth.T),
        both(rows),
        both(rows.transpose(0, 2, 1)),
        both(columns),
        both(columns.transpose(0, 2, 1)),
        symbol_xz,
        symbol_y,
    )


def halves(values):
    top = values.astype(jnp.bfloat16)
    rest = (values - top.astype(jnp.float32)).astype(jnp.bfloat16)
    return top, rest


def dot(left, right):
    return jnp.dot(left, right, preferred_element_type=jnp.float32)


def table_times(table, values):
    top, rest = halves(values)
    return dot(table[0], top) + (dot(table[1], top) + dot(table[0], rest))


def times_table(values, table):
    top, rest = halves(values)
    return dot(top, table[0]) + (dot(rest, table[0]) + dot(top, table[1]))


def outward(step, size):
    odd = lax.rem(step, 2)
    return size // 2 + (1 - odd) * (step // 2) - odd * ((step + 1) // 2)


def exchange_gx(s, t, source, target, own_sem, send_sem, recv_sem):
    own = pltpu.make_async_copy(source.at[pl.ds(3 * s, 3)], target.at[pl.ds(3 * s, 3)], own_sem)
    own.start()

    chip = lax.rem(s // 2, 4)
    beside = [
        2 * lax.rem(chip + dx, 4) + lax.rem(s + dc, 2) for dx in (2, 1, 3, 0) for dc in (1, 0)
    ]

    def send_to(peer):
        pltpu.make_async_remote_copy(
            src_ref=source.at[pl.ds(3 * peer, 3)],
            dst_ref=target.at[pl.ds(3 * s, 3)],
            send_sem=send_sem,
            recv_sem=recv_sem,
            device_id=(peer, t),
            device_id_type=MESH,
        ).start()

    layers = [8 * lax.rem(s // 8 + dz, 8) for dz in range(8)]
    hops = [2, 2, 1, 1, 1, 1, 0, 0]
    order = [(dz, low) for dz in range(8) for low in range(8) if dz or low < 7]
    for dz, low in sorted(order, key=lambda to: -min(to[0], 8 - to[0]) - hops[to[1]]):
        send_to(layers[dz] + beside[low])
    own.wait()
    moved = pl.ds(0, 3 * (GX - 1))
    pltpu.make_async_copy(source.at[moved], target.at[moved], recv_sem).wait()
    pltpu.make_async_copy(source.at[moved], target.at[moved], send_sem).wait()


def exchange_gy(s, t, source, target, own_sem, send_sem, recv_sem):
    own = pltpu.make_async_copy(source.at[pl.ds(32 * t, 32)], target.at[pl.ds(32 * t, 32)], own_sem)
    own.start()

    for dy in (4, 3, 5, 2, 6, 1, 7):
        peer = lax.rem(t + dy, GY)
        pltpu.make_async_remote_copy(
            src_ref=source.at[pl.ds(32 * peer, 27)],
            dst_ref=target.at[pl.ds(32 * t, 27)],
            send_sem=send_sem,
            recv_sem=recv_sem,
            device_id=(s, peer),
            device_id_type=MESH,
        ).start()
    own.wait()
    moved = pl.ds(0, 27 * (GY - 1))
    pltpu.make_async_copy(source.at[moved], target.at[moved], recv_sem).wait()
    pltpu.make_async_copy(source.at[moved], target.at[moved], send_sem).wait()


def dot_across(left, right):
    return lax.dot_general(
        left, right, (((1,), (1,)), ((), ())), preferred_element_type=jnp.float32
    )


def spread_weights(cells, weights, bricks, shown):
    top, rest = halves(weights)
    found = dot_across(cells, top) + dot_across(cells, rest)
    row = lax.broadcasted_iota(jnp.int32, (64, 128), 0)
    mask = (lax.rem(row, 16) // 4 == bricks // 64) & shown
    return [jnp.where(mask, found[64 * k : 64 * k + 64], 0.0) for k in range(4)]


def part_of(star, selector, weights):
    top, rest = halves(star)
    found = dot(top, selector) + dot(rest, selector)
    sums = []
    for c in range(3):
        total = jnp.zeros((64, 128), jnp.float32)
        for k in range(4):
            cell = found[64 * c : 64 * c + 64, 128 * k : 128 * k + 128]
            total = total + cell * weights[k]
        sums.append(jnp.sum(total, axis=0, keepdims=True))
    return jnp.concatenate(sums, axis=0)


def depth_cells(bricks):
    first = 4 * lax.rem(bricks, 64)
    wanted = jnp.concatenate([first + k for k in range(4)], axis=1)
    z = lax.broadcasted_iota(jnp.int32, (256, 512), 0)
    return jnp.where(z == wanted, 1.0, 0.0).astype(jnp.bfloat16)


def spread(impulse, weights, selector):
    terms = jnp.concatenate(
        [
            jnp.concatenate([weights[k] * impulse[c : c + 1] for k in range(4)], axis=1)
            for c in range(3)
        ],
        axis=0,
    )
    top, rest = halves(terms)
    return dot_across(top, selector) + dot_across(rest, selector)


def place_of(px, xi):
    return 2 * xi + 1 - px


def put(padded, start, size, values, stride=None):
    padded[0, pl.ds(start, size, stride)] = values[:, :128]
    padded[1, pl.ds(start, size, stride)] = values[:, 128:]


def take(padded, start, size, stride=None):
    return jnp.concatenate(
        [padded[half, pl.ds(start, size, stride)] for half in range(2)], axis=1
    )


def step_kernel(
    velocity,
    bricks_hbm,
    flags_hbm,
    weights_hbm,
    target_hbm,
    contact_hbm,
    cells_hbm,
    depth_hbm,
    rows_hbm,
    rows_back_hbm,
    columns_hbm,
    columns_back_hbm,
    symbol_xz_hbm,
    symbol_y_hbm,
    forced_out,
    home_out,
    impulse_out,
    bricks,
    flags,
    target_velocity,
    contact_force,
    cells,
    symbol_xz,
    symbol_y,
    depth,
    rows,
    rows_back,
    columns,
    columns_back,
    region,
    weights,
    weights_below,
    bricks_below,
    flags_below,
    wanted,
    wanted_below,
    part_here,
    part_next,
    star,
    impulse_kept,
    forced,
    padded,
    classes,
    line_out,
    line_in,
    y_out,
    x_in,
    x_out,
    y_in,
    line_back,
    line_home,
    table_sem,
    near_send,
    near_recv,
    own_sem,
    send_sem,
    recv_sem,
    save_sem,
):
    s = lax.axis_index("gx")
    t = lax.axis_index("gy")
    px = t // 4
    py = lax.rem(t // 2, 2)
    loads = [
        pltpu.make_async_copy(source, target, table_sem.at[number])
        for number, (source, target) in enumerate(
            (
                (depth_hbm, depth),
                (rows_hbm.at[py], rows),
                (rows_back_hbm.at[py], rows_back),
                (columns_hbm.at[px], columns),
                (columns_back_hbm.at[px], columns_back),
                (velocity, region.at[:, pl.ds(1, 4), pl.ds(8, 16)]),
                (weights_hbm, weights),
                (bricks_hbm, bricks),
                (flags_hbm, flags),
                (target_hbm, target_velocity),
                (contact_hbm, contact_force),
                (cells_hbm, cells),
                (symbol_xz_hbm, symbol_xz),
                (symbol_y_hbm.at[pl.ds(s, 1)], symbol_y),
            )
        )
    ]
    for number in (7, 8, 11, 6, 5, 9, 10, 0, 1, 3, 4, 12, 13, 2):
        loads[number].start()
    line_in[...] = jnp.zeros_like(line_in)
    barrier = pltpu.get_barrier_semaphore()

    def away(dx, dy):
        return (lax.rem(s + GX + dx, GX), lax.rem(t + GY + dy, GY))

    chip = lax.rem(s // 2, 4)
    beside = [
        2 * lax.rem(chip + dx, 4) + lax.rem(s + dc, 2) for dx in (2, 1, 3, 0) for dc in (1, 0)
    ]

    def greet(where):
        pl.semaphore_signal(barrier, inc=1, device_id=where, device_id_type=MESH)

    def greet_layer(step, carry):
        layer = 8 * lax.rem(s // 8 + outward(step, 8), 8)
        for low in beside:
            greet((layer + low, t))
        return carry

    lax.fori_loop(0, 7, greet_layer, 0)
    for low in beside[:7]:
        greet((8 * (s // 8) + low, t))
    for dy in (4, 3, 5, 2, 6, 1, 7):
        greet((s, lax.rem(t + dy, GY)))
    pl.semaphore_wait(barrier, GX - 1 + GY - 1)

    near = [
        pltpu.make_async_remote_copy(
            src_ref=source,
            dst_ref=target,
            send_sem=near_send.at[number],
            recv_sem=near_recv.at[number],
            device_id=away(*where),
            device_id_type=MESH,
        )
        for number, (source, target, where) in enumerate(
            (
                (velocity.at[:, :, pl.ds(0, 1)], region.at[:, pl.ds(1, 4), pl.ds(24, 1)], (0, -1)),
                (velocity.at[:, :, pl.ds(15, 1)], region.at[:, pl.ds(1, 4), pl.ds(7, 1)], (0, 1)),
                (velocity.at[:, pl.ds(0, 1)], region.at[:, pl.ds(5, 1), pl.ds(8, 16)], (-1, 0)),
                (velocity.at[:, pl.ds(3, 1)], region.at[:, pl.ds(0, 1), pl.ds(8, 16)], (1, 0)),
                (bricks_hbm, bricks_below, (1, 0)),
                (flags_hbm, flags_below, (1, 0)),
                (weights_hbm, weights_below, (1, 0)),
                (wanted, wanted_below, (1, 0)),
                (part_here, part_next, (-1, 0)),
            )
        )
    ]
    for number in range(7):
        near[number].start()

    for number in (7, 8, 11, 6):
        loads[number].wait()
    live = flags[...] > 0
    own_weights = spread_weights(cells[0:256], weights[...], bricks[...], live)
    selector = depth_cells(bricks[...])
    for number in (4, 5, 6):
        near[number].wait_recv()
    here_weights = spread_weights(
        cells[256:512], weights_below[...], bricks_below[...], flags_below[...] == 2
    )
    selector_below = depth_cells(bricks_below[...])
    for number in (5, 9, 10):
        loads[number].wait()
    for number in range(4):
        near[number].wait_recv()
    for x in range(1, 5):
        centers = [region[c, x, 8:24] for c in range(3)]
        for c in range(3):
            v = centers[c]
            uppers = (region[c, x + 1, 8:24], region[c, x, 9:25], pltpu.roll(v, 255, 1))
            lowers = (region[c, x - 1, 8:24], region[c, x, 7:23], pltpu.roll(v, 1, 1))
            laplace = -6.0 * v
            carried = jnp.zeros_like(v)
            for d in range(3):
                laplace = laplace + (uppers[d] + lowers[d])
                carried = carried + centers[d] * (uppers[d] - lowers[d])
            base = 64 * c + 16 * (x - 1)
            star[base : base + 16] = v + time_step * (viscosity * laplace - 0.5 * carried)

    part_here[...] = part_of(star[...], selector_below, here_weights)
    near[8].start()
    wanted[...] = (
        target_velocity[...]
        + time_step * contact_force[...]
        - part_of(star[...], selector, own_weights)
    )
    near[7].start()
    near[7].wait_recv()
    near[8].wait_recv()
    impulse = jnp.where(live, wanted[...] - part_next[...], 0.0)
    impulse_below = jnp.where(flags_below[...] > 0, wanted_below[...] - part_here[...], 0.0)
    impulse_kept[...] = impulse
    at_home = spread(impulse, own_weights, selector)
    from_below = spread(impulse_below, here_weights, selector_below)
    for c in range(3):
        for x in range(4):
            base = 64 * c + 16 * x
            forced[c, x] = star[base : base + 16] + volume_ratio * (
                at_home[base : base + 16] + from_below[base : base + 16]
            )

    saved = [
        pltpu.make_async_copy(impulse_kept, impulse_out, save_sem.at[0]),
        pltpu.make_async_copy(forced, forced_out, save_sem.at[1]),
    ]
    for copy in saved:
        copy.start()

    classes[...] = jnp.zeros_like(classes)
    row_number = lax.broadcasted_iota(jnp.int32, (16, 256), 0)
    for place in range(6):
        x = place - 1
        total = jnp.zeros((16, 256), jnp.float32)
        if 0 <= x + 1 < 4:
            total = total + forced[0, x + 1]
        if 0 <= x - 1 < 4:
            total = total - forced[0, x - 1]
        if 0 <= x < 4:
            v = forced[1, x]
            w = forced[2, x]
            upper = jnp.where(row_number == 15, 0.0, pltpu.roll(v, 15, 0))
            lower = jnp.where(row_number == 0, 0.0, pltpu.roll(v, 1, 0))
            total = total + (upper - lower)
            total = total + (pltpu.roll(w, 255, 1) - pltpu.roll(w, 1, 1))
            put(padded, 32 * place + 7, 1, 0.5 * forced[1, x, 0:1])
            put(padded, 32 * place + 24, 1, -0.5 * forced[1, x, 15:16])
        else:
            put(padded, 32 * place + 7, 1, jnp.zeros((1, 256), jnp.float32))
            put(padded, 32 * place + 24, 1, jnp.zeros((1, 256), jnp.float32))
        put(padded, 32 * place + 8, 16, 0.5 * total)
    for a in range(2):
        for b in range(2):
            base = 32 * (2 * a + b)
            for xi in range(3):
                place = 32 * place_of(a, xi)
                classes[base + 8 * xi : base + 8 * xi + 8] = take(padded, place + 8 + b, 8, 2)
                edge = place + (7 if b else 24)
                classes[base + 24 + xi : base + 25 + xi] = take(padded, edge, 1)
    loads[0].wait()
    spectrum = times_table(classes[...], depth)
    for c in range(8):
        line_out[32 * c : 32 * c + 32] = spectrum[
            32 * (c // 2) : 32 * (c // 2) + 32, 128 * (c % 2) : 128 * (c % 2) + 128
        ]
    exchange_gy(s, t, line_out, line_in, own_sem.at[0], send_sem.at[0], recv_sem.at[0])

    loads[1].wait()
    y_out[...] = table_times(rows, line_in[...])
    exchange_gx(s, t, y_out, x_in, own_sem.at[1], send_sem.at[1], recv_sem.at[1])

    for number in (3, 4, 12, 13):
        loads[number].wait()
    symbol = symbol_xz[...] + symbol_y[...]
    positive = symbol > 0
    factor = jnp.where(positive, -1.0 / jnp.where(positive, symbol, 1.0), 0.0)
    x_out[...] = table_times(columns_back, table_times(columns, x_in[...]) * factor)
    exchange_gx(s, t, x_out, y_in, own_sem.at[2], send_sem.at[2], recv_sem.at[2])

    loads[2].wait()
    line_back[...] = table_times(rows_back, y_in[...])
    exchange_gy(s, t, line_back, line_home, own_sem.at[3], send_sem.at[3], recv_sem.at[3])

    saved.append(pltpu.make_async_copy(line_home, home_out, save_sem.at[2]))
    saved[2].start()
    for copy in saved:
        copy.wait()
    for copy in near:
        copy.wait_send()


def finish_kernel(
    home_hbm,
    depth_back_hbm,
    forced_hbm,
    impulse_hbm,
    velocity_out,
    potential_out,
    impulse_out,
    line_home,
    depth_back,
    forced,
    classes,
    padded,
    potential,
    velocity_new,
    load_sem,
    save_sem,
):
    loads = [
        pltpu.make_async_copy(source, target, load_sem.at[number])
        for number, (source, target) in enumerate(
            ((home_hbm, line_home), (depth_back_hbm, depth_back), (forced_hbm, forced))
        )
    ]
    for load in loads:
        load.start()
    saves = [
        pltpu.make_async_copy(source, target, save_sem.at[number])
        for number, (source, target) in enumerate(
            (
                (impulse_hbm, impulse_out),
                (potential, potential_out),
                (velocity_new.at[0], velocity_out.at[0]),
                (velocity_new.at[1], velocity_out.at[1]),
                (velocity_new.at[2], velocity_out.at[2]),
            )
        )
    ]
    saves[0].start()
    loads[0].wait()
    loads[1].wait()
    home = jnp.concatenate(
        [
            jnp.concatenate(
                [line_home[64 * c : 64 * c + 32], line_home[64 * c + 32 : 64 * c + 64]], axis=1
            )
            for c in range(4)
        ],
        axis=0,
    )
    classes[...] = times_table(home, depth_back)
    for a in range(2):
        for b in range(2):
            base = 32 * (2 * a + b)
            for xi in range(3):
                place = 32 * place_of(a, xi)
                put(padded, place + 8 + b, 8, classes[base + 8 * xi : base + 8 * xi + 8], 2)
                edge = place + (7 if b else 24)
                put(padded, edge, 1, classes[base + 24 + xi : base + 25 + xi])
    for x in range(4):
        potential[x] = take(padded, 32 * x + 40, 16)
    saves[1].start()
    loads[2].wait()
    for x in range(4):
        base = 32 * (x + 1)
        velocity_new[0, x] = forced[0, x] - 0.5 * (
            take(padded, base + 40, 16) - take(padded, base - 24, 16)
        )
    saves[2].start()
    for x in range(4):
        base = 32 * (x + 1)
        velocity_new[1, x] = forced[1, x] - 0.5 * (
            take(padded, base + 9, 16) - take(padded, base + 7, 16)
        )
    saves[3].start()
    for x in range(4):
        p = potential[x]
        velocity_new[2, x] = forced[2, x] - 0.5 * (pltpu.roll(p, 255, 1) - pltpu.roll(p, 1, 1))
    saves[4].start()
    for save in saves:
        save.wait()


def step(velocity, owner_brick, particle_flags, weights, target_velocity, contact_force):
    tables = list(build_tables())
    outside = pl.BlockSpec(memory_space=pltpu.HBM)
    f32, bf16 = jnp.float32, jnp.bfloat16
    depth_back = jnp.asarray(tables.pop(2))
    forced, home, impulse = pl.pallas_call(
        step_kernel,
        out_shape=(
            jax.ShapeDtypeStruct((3, 4, 16, 256), f32),
            jax.ShapeDtypeStruct((256, 128), f32),
            jax.ShapeDtypeStruct((3, 128), f32),
        ),
        in_specs=[outside] * 14,
        out_specs=(outside, outside, outside),
        scratch_shapes=[
            pltpu.VMEM((1, 128), jnp.int32),
            pltpu.VMEM((1, 128), jnp.int32),
            pltpu.VMEM((3, 128), f32),
            pltpu.VMEM((3, 128), f32),
            pltpu.VMEM((512, 128), bf16),
            pltpu.VMEM((128, 128), f32),
            pltpu.VMEM((1, 128), f32),
            pltpu.VMEM((2, 256, 256), bf16),
            pltpu.VMEM((2, 192, 256), bf16),
            pltpu.VMEM((2, 256, 192), bf16),
            pltpu.VMEM((2, 128, 192), bf16),
            pltpu.VMEM((2, 192, 128), bf16),
            pltpu.VMEM((3, 6, 32, 256), f32),
            pltpu.VMEM((128, 128), f32),
            pltpu.VMEM((128, 128), f32),
            pltpu.VMEM((1, 128), jnp.int32),
            pltpu.VMEM((1, 128), jnp.int32),
            pltpu.VMEM((3, 128), f32),
            pltpu.VMEM((3, 128), f32),
            pltpu.VMEM((3, 128), f32),
            pltpu.VMEM((3, 128), f32),
            pltpu.VMEM((192, 256), f32),
            pltpu.VMEM((3, 128), f32),
            pltpu.VMEM((3, 4, 16, 256), f32),
            pltpu.VMEM((2, 192, 128), f32),
            pltpu.VMEM((128, 256), f32),
            pltpu.VMEM((256, 128), f32),
            pltpu.VMEM((256, 128), f32),
            pltpu.VMEM((192, 128), f32),
            pltpu.VMEM((192, 128), f32),
            pltpu.VMEM((192, 128), f32),
            pltpu.VMEM((192, 128), f32),
            pltpu.VMEM((256, 128), f32),
            pltpu.VMEM((256, 128), f32),
            pltpu.SemaphoreType.DMA((14,)),
            pltpu.SemaphoreType.DMA((9,)),
            pltpu.SemaphoreType.DMA((9,)),
            pltpu.SemaphoreType.DMA((4,)),
            pltpu.SemaphoreType.DMA((4,)),
            pltpu.SemaphoreType.DMA((4,)),
            pltpu.SemaphoreType.DMA((3,)),
        ],
        compiler_params=pltpu.CompilerParams(
            collective_id=0, has_side_effects=True, vmem_limit_bytes=60 * 1024 * 1024
        ),
    )(
        velocity,
        owner_brick.reshape(1, 128),
        particle_flags.reshape(1, 128),
        weights,
        target_velocity,
        contact_force,
        *[jnp.asarray(table) for table in tables],
    )
    return pl.pallas_call(
        finish_kernel,
        out_shape=(
            jax.ShapeDtypeStruct((3, 4, 16, 256), f32),
            jax.ShapeDtypeStruct((4, 16, 256), f32),
            jax.ShapeDtypeStruct((3, 128), f32),
        ),
        in_specs=[outside] * 4,
        out_specs=(outside, outside, outside),
        scratch_shapes=[
            pltpu.VMEM((256, 128), f32),
            pltpu.VMEM((2, 256, 256), bf16),
            pltpu.VMEM((3, 4, 16, 256), f32),
            pltpu.VMEM((128, 256), f32),
            pltpu.VMEM((2, 192, 128), f32),
            pltpu.VMEM((4, 16, 256), f32),
            pltpu.VMEM((3, 4, 16, 256), f32),
            pltpu.SemaphoreType.DMA((3,)),
            pltpu.SemaphoreType.DMA((5,)),
        ],
        compiler_params=pltpu.CompilerParams(vmem_limit_bytes=60 * 1024 * 1024),
    )(home, depth_back, forced, impulse)


def solution(mesh):
    placed = (
        P(None, "gx", "gy", None),
        P(("gx", "gy")),
        P(("gx", "gy")),
        P(("gx", "gy"), None),
        P(None, ("gx", "gy")),
        P(None, ("gx", "gy")),
    )
    return jax.shard_map(
        step,
        mesh=mesh,
        in_specs=placed,
        out_specs=(P(None, "gx", "gy", None), P("gx", "gy", None), P(None, ("gx", "gy"))),
        check_vma=False,
    )
```
